256 devices in a mesh: mem: 8 (over y_lo, x), tile: 32 (over z, y_hi, core).
Axes of the slice: x: 4, y: 4 (y_hi: 2, y_lo: 2; y = y_hi * 2 + y_lo), z: 8, core: 2. Of those that a mesh axis runs over, the one named last changes fastest.
Arguments:
- prior_moisture_sample: float32 [256, 4, 131072], P('mem', None, 'tile'), may hold values from -6 to 6
- measurement_matrix: float32 [4, 64, 32], replicated, may hold values from -0.375 to 0.375
- measured_window_readings: float32 [2048, 32], P(('tile', 'mem')), may hold values from -6 to 6
- measurement_noise_spread: float32 [2048, 32], P(('tile', 'mem')), may hold values from 1 to 4
- nearby_window_indices: int32 [4096, 8], P(('tile', 'mem')), may hold values from 0 to 2047, as said below
- window_damping_weight: int32 [4096, 8], P(('tile', 'mem')), may hold values from 0 to 3
Outputs:
- analysis: float32 [256, 4, 131072], P(None, None, ('tile', 'mem'))
The draws below stay inside these ranges and needn't reach their ends.
Inputs may be any that keep to these rules, and one draw needn't show every extreme that they name: `nearby_window_indices`: entry 0 of group g's list is the block of its own cells, g * 32 // 64; every entry is a block of the same tile of 64 consecutive blocks as entry 0 or of a tile next to it.
All inputs are finite; a program needn't handle non-finite values. Where the reference program divides by a largest or mean magnitude, that divisor is 1e-20 or more.
Results may differ from the reference program's by a relative error of at most 0.00011.
Values sent between devices are 32-bit elements; how exact they have to be, the bound alone decides.
No kernel may reach another device: no remote copies, remote signals or barrier semaphores. Data moves between devices by JAX's collectives and lax.ppermute only.
A program may use at most 128 MiB of HBM per device.

```python
import math
import jax
import jax.numpy as jnp
from jax import lax

MEMBER_COUNT = 256
DEPTH_LEVELS = 4
BLOCK = 64
CLUSTER_SITES = 32
OBS = 32
LOC = 8
TAPS = 4
NS_ITERS = 4
BLOCKS_TILE = 64
NBLOCK = 2048
GRID_SITES = 131072
CLUSTER_COUNT = 4096


def draw_nearby_window_indices(key, part):
    key = jax.random.fold_in(key, 17)
    tile_key, block_key = jax.random.split(key)
    groups = jnp.arange(CLUSTER_COUNT, dtype=jnp.int32)
    own_block = groups * CLUSTER_SITES // BLOCK
    tile_count = NBLOCK // BLOCKS_TILE
    own_tile = own_block // BLOCKS_TILE
    tile_step = jax.random.randint(tile_key, (CLUSTER_COUNT, LOC - 1), -1, 2, dtype=jnp.int32)
    chosen_tile = jnp.clip(own_tile[:, None] + tile_step, 0, tile_count - 1)
    within = jax.random.randint(block_key, (CLUSTER_COUNT, LOC - 1), 0, BLOCKS_TILE, dtype=jnp.int32)
    return jnp.concatenate([own_block[:, None], chosen_tile * BLOCKS_TILE + within], axis=1).astype(jnp.int32)


def set_ends(drawn, stream_key, least, high):
    extent = drawn.shape
    place = [jax.random.randint(jax.random.fold_in(stream_key, axis), (), 0, extent[axis]) for axis in range(len(extent))]
    drawn = drawn.at[tuple(place)].set(least)
    longest = extent.index(max(extent))
    place[longest] = (place[longest] + 1) % extent[longest]
    return drawn.at[tuple(place)].set(high)


def shard_levels(own_key, dims, cuts, smallest, high):
    def one(position, shards_of):
        heights = jax.random.uniform(jax.random.fold_in(jax.random.fold_in(own_key, 6), position), (shards_of,), jnp.float32, smallest / len(cuts), high / len(cuts))
        return jnp.repeat(jnp.exp(heights), dims[position] // shards_of).reshape((-1,) + (1,) * (len(dims) - position - 1))

    level = one(*cuts[0])
    for cut in cuts[1:]:
        level = level * one(*cut)
    return level


def bell_draw(key, dims, deviation, most, cuts=(), kind=jnp.bfloat16):
    entries = deviation * jax.random.normal(key, dims, jnp.float32)
    if cuts:
        entries = entries * shard_levels(key, dims, cuts, -0.22, 0.18)
    return jnp.clip(entries, -most, most).astype(kind)


def setup_inputs(seed: int = 0) -> dict:
    streams_of = jax.random.split(jax.random.key(seed), 7)
    prior_moisture_sample = bell_draw(streams_of[0], (MEMBER_COUNT, DEPTH_LEVELS, GRID_SITES), 1.0, 6.0, ((0, 8), (2, 32)), jnp.float32)
    measurement_matrix = bell_draw(streams_of[1], (DEPTH_LEVELS, BLOCK, OBS), (DEPTH_LEVELS * BLOCK) ** -0.5, 0.375, (), jnp.float32)
    measured_window_readings = bell_draw(streams_of[2], (NBLOCK, OBS), 1.5, 6.0, ((0, 256),), jnp.float32)
    measurement_noise_spread = jnp.clip(jnp.exp(math.log(4.0) - 1.3862944 * jax.random.uniform(streams_of[3], (NBLOCK, OBS), jnp.float32) ** shard_levels(streams_of[3], (NBLOCK, OBS), ((0, 256),), -0.2, 0.2)), 1.0, 4.0)
    nearby_window_indices = draw_nearby_window_indices(jax.random.fold_in(streams_of[6], 71), 0)
    window_damping_weight = set_ends(jax.random.randint(streams_of[5], (CLUSTER_COUNT, LOC), 0, TAPS), jax.random.fold_in(streams_of[5], 1), 0, TAPS - 1).astype(jnp.int32)
    return dict(prior_moisture_sample=prior_moisture_sample, measurement_matrix=measurement_matrix, measured_window_readings=measured_window_readings, measurement_noise_spread=measurement_noise_spread, nearby_window_indices=nearby_window_indices, window_damping_weight=window_damping_weight)


precise = lax.Precision.HIGHEST

def forward_model_action(sample_moisture_field, measurement_matrix):
    members, layers, cell_count = sample_moisture_field.shape
    blocks = cell_count // measurement_matrix.shape[1]
    shaped = sample_moisture_field.reshape(members, layers, blocks, measurement_matrix.shape[1])
    values = jnp.einsum('klbc,lcp->kbp', shaped, measurement_matrix, precision=precise)
    return values.reshape(members, blocks * measurement_matrix.shape[2])

def transform(obs_part, misfit_part, weights):
    members = obs_part.shape[0]
    identity = jnp.eye(members, dtype=jnp.float32)
    weighted = obs_part * weights[None]
    precision_mat = (members - 1.0) * identity + jnp.einsum('jgo,kgo->gjk', weighted, obs_part, precision=precise)
    obs_drive = jnp.einsum('jgo,go->gj', weighted, misfit_part, precision=precise)
    row_bound = lax.optimization_barrier(jnp.max(lax.optimization_barrier(jnp.sum(jnp.abs(precision_mat), axis=2)), axis=1))
    current = precision_mat / row_bound[:, None, None]
    root_inv = jnp.broadcast_to(identity, precision_mat.shape)
    for sweep_index in range(NS_ITERS):
        product = jnp.einsum('gij,gjk->gik', root_inv, current, precision=precise)
        factor = 1.5 * identity - 0.5 * product
        current = jnp.einsum('gij,gjk->gik', current, factor, precision=precise)
        root_inv = jnp.einsum('gij,gjk->gik', factor, root_inv, precision=precise)
    inner_drive = jnp.einsum('gjk,gk->gj', root_inv, obs_drive, precision=precise)
    offset = jnp.einsum('gjk,gk->gj', root_inv, inner_drive, precision=precise) / row_bound[:, None]
    return jnp.sqrt((members - 1.0) / row_bound)[:, None, None] * root_inv + offset[:, :, None]

def apply_mixing(sample_moisture_field, mixing):
    average = lax.optimization_barrier(jnp.mean(sample_moisture_field, axis=0))
    return average + jnp.einsum('jlgc,gjk->klgc', sample_moisture_field - average, mixing, precision=precise)

def reference(prior_moisture_sample, measurement_matrix, measured_window_readings, measurement_noise_spread, nearby_window_indices, window_damping_weight):
    forward_model_outputs = forward_model_action(prior_moisture_sample, measurement_matrix)
    obs_mean = lax.optimization_barrier(jnp.mean(forward_model_outputs, axis=0))
    inv_scale = 1.0 / jnp.sqrt(measurement_noise_spread.reshape(-1))
    scaled = (forward_model_outputs - obs_mean) * inv_scale
    misfit = (measured_window_readings.reshape(-1) - obs_mean) * inv_scale
    columns = (nearby_window_indices[:, :, None] * OBS + jnp.arange(OBS, dtype=jnp.int32)).astype(jnp.int32)
    columns = columns.reshape(CLUSTER_COUNT, LOC * OBS)
    weights = jnp.repeat(1.0 / (1.0 + window_damping_weight.astype(jnp.float32)), OBS, axis=1)
    cluster_wise_outputs = math.gcd(CLUSTER_COUNT, 16)
    cluster_sorted_prior = prior_moisture_sample.reshape(MEMBER_COUNT, DEPTH_LEVELS, CLUSTER_COUNT // cluster_wise_outputs, cluster_wise_outputs, CLUSTER_SITES)
    cluster_sorted_prior = jnp.moveaxis(cluster_sorted_prior, 2, 0)

    def one_batch(pieces):
        sample_moisture_field, batch_columns, batch_weights = pieces
        obs_part = jnp.take(scaled, batch_columns, axis=1)
        mixing = transform(obs_part, misfit[batch_columns], batch_weights)
        return apply_mixing(sample_moisture_field, mixing)
    result = lax.map(one_batch, (cluster_sorted_prior, columns.reshape(CLUSTER_COUNT // cluster_wise_outputs, cluster_wise_outputs, LOC * OBS), weights.reshape(CLUSTER_COUNT // cluster_wise_outputs, cluster_wise_outputs, LOC * OBS)))
    return jnp.moveaxis(result, 0, 2).reshape(MEMBER_COUNT, DEPTH_LEVELS, GRID_SITES)
```

```python
import jax
import jax.numpy as jnp
from jax import lax
from jax.experimental import pallas as pl
from jax.experimental.pallas import tpu as pltpu
from jax.sharding import PartitionSpec as P

F32 = jnp.float32
BF16 = jnp.bfloat16
MEM = 8
LANES = 128


def split(x):
    hi = x.astype(BF16)
    lo = (x - hi.astype(F32)).astype(BF16)
    return hi, lo


def dot(a, b):
    return jnp.dot(a, b, preferred_element_type=F32)


def dot_nt(a, b):
    return lax.dot_general(a, b, (((1,), (1,)), ((), ())), preferred_element_type=F32)


def mul3(a, b):
    (ah, al), (bh, bl) = a, b
    return dot(ah, bh) + (dot(ah, bl) + dot(al, bh))


def exchange_lanes(parts, first, second):
    out = list(parts)
    for bit, shift, odd in ((1, 32, first), (2, 64, second)):
        for low in range(4):
            if low & bit:
                continue
            a, b = out[low], out[low | bit]
            out[low] = jnp.where(odd, pltpu.roll(b, shift, 1), a)
            out[low | bit] = jnp.where(odd, b, pltpu.roll(a, LANES - shift, 1))
    return out


def lane_bits(rows):
    lane = lax.broadcasted_iota(jnp.int32, (rows, LANES), 1)
    return (lane // 32) % 2 == 1, lane // 64 == 1


def obs_kernel(where_ref, prior_ref, map_ref, extra_ref, *refs):
    pieces, obs_ref, stack = refs[:MEM], refs[MEM], refs[MEM + 1]
    members = prior_ref.shape[0]
    me = where_ref[0]
    first, second = lane_bits(members)
    for s in range(MEM):
        peer = me ^ s
        for c in range(4):
            base = pl.multiple_of(peer * 512 + c * LANES, LANES)
            layers = [prior_ref[:, l, pl.ds(base, LANES)] for l in range(4)]
            groups = exchange_lanes(layers, first, second)
            for g in range(4):
                at = c * 4 + g
                pieces[s][:, at * LANES : (at + 1) * LANES] = groups[g]
                row = pl.multiple_of((peer * 2 + at // 8) * members, members)
                stack[pl.ds(row, members), (at % 8) * LANES : (at % 8 + 1) * LANES] = groups[g]
    halves = [map_ref[l, 32 * h : 32 * h + 32, :] for h in range(2) for l in range(4)]
    tall = jnp.concatenate(halves, axis=0)
    wide = jnp.concatenate([tall] * 4, axis=1)
    big = jnp.concatenate([wide] * 4, axis=0)
    row = lax.broadcasted_iota(jnp.int32, big.shape, 0)
    lane = lax.broadcasted_iota(jnp.int32, big.shape, 1)
    weights = jnp.where(row // 256 == lane // 32, big, 0.0)
    values = mul3(split(stack[...]), split(weights))
    for q in range(16):
        obs_ref[:, q * LANES : (q + 1) * LANES] = values[q * members : (q + 1) * members]
    obs_ref[0:8, 2048:2176] = extra_ref[...]
    obs_ref[8:, 2048:2176] = jnp.zeros((members - 8, LANES), F32)


def local_obs(where, prior, measurement_matrix, extra):
    members = prior.shape[0]
    vmem = pl.BlockSpec(memory_space=pltpu.VMEM)
    return pl.pallas_call(
        obs_kernel,
        out_shape=[jax.ShapeDtypeStruct((members, 2048), F32)] * MEM
        + [jax.ShapeDtypeStruct((members, 2176), F32)],
        in_specs=[pl.BlockSpec(memory_space=pltpu.SMEM), vmem, vmem, vmem],
        out_specs=[vmem] * (MEM + 1),
        scratch_shapes=[pltpu.VMEM((512, 1024), F32)],
        compiler_params=pltpu.CompilerParams(vmem_limit_bytes=48 << 20),
        name="local_obs",
    )(where, prior, measurement_matrix, extra)


def square(p):
    h, l = p
    m = dot(h, l)
    return dot(h, h) + (m + dot(l, h))


def analysis_kernel(*refs):
    where_ref, column_ref, weight_ref = refs[:3]
    pieces = refs[3 : 3 + MEM]
    obs = refs[3 + MEM : 3 + MEM + 9]
    out_ref = refs[3 + MEM + 9]
    raw, table, field, sems = refs[3 + MEM + 10 :]
    me = where_ref[0]
    own, g1, g3, g2o, g2h, sib, sib1, sib3, sib2 = obs
    copies = []

    def place(source, row, slot, peer):
        copies.append(
            pltpu.make_async_copy(
                source.at[pl.ds(row, 32), :],
                raw.at[slot, pl.ds(pl.multiple_of(peer * 32, 32), 32), :],
                sems.at[len(copies)],
            )
        )

    for source, x in ((own, 0), (g1, 1), (g3, 3)):
        for half in range(2):
            for y in range(2):
                place(source, half * 64 + y * 32, 2 * half, me ^ x ^ (4 * y))
    for source, slot in ((g2o, 0), (g2h, 2)):
        for y in range(2):
            place(source, y * 32, slot, me ^ 2 ^ (4 * y))
    for source, x in ((sib, 0), (sib1, 1), (sib3, 3), (sib2, 2)):
        for y in range(2):
            place(source, y * 32, 1, me ^ x ^ (4 * y))
    for copy in copies:
        copy.start()
    total = jnp.zeros((1, 2048), F32)
    for s in range(MEM):
        row = pl.multiple_of((me ^ s) * 32, 32)
        value = pieces[s][...]
        field[pl.ds(row, 32), :] = value
        total = total + jnp.sum(value, axis=0, keepdims=True)
    field[256:257, :] = total * (1.0 / 256.0)
    for copy in copies:
        copy.wait()
    for slot in range(3):
        extras = [raw[slot, 32 * m : 32 * m + 8, 2048:2176] for m in range(MEM)]
        reading = jnp.concatenate([e[i : i + 1] for e in extras for i in (0, 1)], axis=1)
        spread = jnp.concatenate([e[i : i + 1] for e in extras for i in (2, 3)], axis=1)
        scale = 1.0 / jnp.sqrt(spread)
        value = raw[slot, :, 0:2048]
        mean = jnp.sum(value, axis=0, keepdims=True) * (1.0 / 256.0)
        table[0:256, slot * 2048 : (slot + 1) * 2048] = (value - mean) * scale
        table[256:264, slot * 2048 : (slot + 1) * 2048] = jnp.broadcast_to(
            (reading - mean) * scale, (8, 2048)
        )

    rows = lax.broadcasted_iota(jnp.int32, (256, 256), 0)
    cols = lax.broadcasted_iota(jnp.int32, (256, 256), 1)
    diagonal = rows == cols
    block = lax.broadcasted_iota(jnp.int32, (1, LANES), 1) // 32

    def pick(g):
        halves = []
        for h in range(2):
            piece = jnp.zeros((264, LANES), F32)
            factor = jnp.zeros((1, LANES), F32)
            for i in range(4):
                place_at = column_ref[g * 8 + 4 * h + i]
                base = pl.multiple_of((place_at // 4) * LANES, LANES)
                shift = lax.rem(i - lax.rem(place_at, 4) + 4, 4) * 32
                moved = pltpu.roll(table[:, pl.ds(base, LANES)], shift, 1)
                piece = jnp.where(block == i, moved, piece)
                factor = jnp.where(block == i, weight_ref[g * 8 + 4 * h + i], factor)
            halves.append(piece * factor)
        return jnp.concatenate(halves, axis=1)

    def one(g):
        both = pick(g)
        chosen = both[0:256]
        drive = jnp.sum(chosen * both[256:257], axis=1, keepdims=True)
        h, l = split(chosen)
        gram = dot_nt(h, h) + (dot_nt(h, l) + dot_nt(l, h))
        precision = gram + jnp.where(diagonal, 255.0, 0.0)
        bound = jnp.max(jnp.sum(jnp.abs(precision), axis=0, keepdims=True), axis=1, keepdims=True)
        inverse = 1.0 / bound
        first = precision * inverse
        roots = []
        current = first
        for step in range(3):
            parts = split(current)
            second = square(parts)
            if step != 1:
                mixed = split(second - 4.5 * current)
                roots.append(
                    0.0625 * square(mixed)
                    + (0.421875 * second - 2.4375 * current + jnp.where(diagonal, 2.25, 0.0))
                )
            if step < 2:
                current = 2.25 * current - 1.5 * second + 0.25 * mul3(parts, split(second))
        root = mul3(split(roots[0]), split(roots[1]))
        inner = jnp.sum(root * drive, axis=0, keepdims=True)
        offset = jnp.sum(root * inner, axis=1, keepdims=True) * inverse
        at = pl.multiple_of(g * LANES, LANES)
        average = field[256:257, pl.ds(at, LANES)]
        anomaly = field[0:256, pl.ds(at, LANES)] - average
        base = average + jnp.sum(anomaly * offset, axis=0, keepdims=True)
        spread = mul3(split(root), split(anomaly))
        field[0:256, pl.ds(at, LANES)] = base + jnp.sqrt(255.0 * inverse) * spread

    def pair(i, carry):
        one(2 * i)
        one(2 * i + 1)
        return carry

    lax.fori_loop(0, 8, pair, 0)
    odd, high = lane_bits(256)
    for c in range(4):
        groups = [field[0:256, (4 * c + g) * LANES : (4 * c + g + 1) * LANES] for g in range(4)]
        layers = exchange_lanes(groups, odd, high)
        for l in range(4):
            out_ref[:, l, c * LANES : (c + 1) * LANES] = layers[l]


def analyse(where, columns, weights, pieces, obs):
    vmem = pl.BlockSpec(memory_space=pltpu.VMEM)
    smem = pl.BlockSpec(memory_space=pltpu.SMEM)
    anywhere = pl.BlockSpec(memory_space=pl.ANY)
    return pl.pallas_call(
        analysis_kernel,
        out_shape=jax.ShapeDtypeStruct((256, 4, 512), F32),
        in_specs=[smem] * 3 + [vmem] * MEM + [anywhere] * 9,
        out_specs=vmem,
        scratch_shapes=[
            pltpu.VMEM((3, 256, 2176), F32),
            pltpu.VMEM((264, 6144), F32),
            pltpu.VMEM((264, 2048), F32),
            pltpu.SemaphoreType.DMA((24,)),
        ],
        compiler_params=pltpu.CompilerParams(vmem_limit_bytes=52 << 20),
        name="analysis",
    )(where, columns, weights, *pieces, *obs)


def send(x, flip):
    return lax.ppermute(x, "mem", [(i, i ^ flip) for i in range(MEM)])


def swap_cores(x):
    return lax.ppermute(x, "tile", [(i, i ^ 1) for i in range(32)])


def local(prior, measurement_matrix, readings, noise, nearby, damping):
    me = lax.axis_index("mem").astype(jnp.int32)
    tile = lax.axis_index("tile").astype(jnp.int32)
    where = jnp.stack([me, tile])
    extra = jnp.concatenate(
        [readings.reshape(2, 128), noise.reshape(2, 128), jnp.zeros((4, 128), F32)], axis=0
    )
    *pieces, obs = local_obs(where, prior, measurement_matrix, extra)
    outer = lax.ppermute(
        obs,
        "tile",
        [(i, i + 1) for i in range(1, 31, 2)] + [(i + 1, i) for i in range(1, 31, 2)],
    )
    across = [send(obs, 4), None]
    across[1] = send(outer, 4)
    own = jnp.concatenate([obs, across[0], outer, across[1]], axis=0)
    g1 = send(own, 1)
    g3 = send(own, 3)
    g2o = send(g3[:64], 1)
    g2h = send(g1[64:], 3)
    sib = swap_cores(own[:64])
    sib1 = swap_cores(g1[:64])
    sib3 = swap_cores(g3[:64])
    sib2 = swap_cores(g2o)
    got = [pieces[0]] + [send(pieces[s], s) for s in range(1, MEM)]
    block_tile = nearby // 64
    slot = jnp.where(block_tile == tile, 0, jnp.where(block_tile // 2 == tile // 2, 1, 2))
    columns = (slot * 64 + nearby % 64).reshape(-1)
    weights = jnp.sqrt(1.0 / (1.0 + damping.astype(F32))).reshape(-1)
    return analyse(where, columns, weights, got, (own, g1, g3, g2o, g2h, sib, sib1, sib3, sib2))


def solution(mesh):
    in_specs = (
        P("mem", None, "tile"),
        P(),
        P(("tile", "mem"), None),
        P(("tile", "mem"), None),
        P(("tile", "mem"), None),
        P(("tile", "mem"), None),
    )
    out_specs = P(None, None, ("tile", "mem"))
    return jax.shard_map(local, mesh=mesh, in_specs=in_specs, out_specs=out_specs, check_vma=False)
```

```python
import jax
import jax.numpy as jnp
from jax import lax
from jax.experimental import pallas as pl
from jax.experimental.pallas import tpu as pltpu
from jax.sharding import PartitionSpec as P

F32 = jnp.float32
BF16 = jnp.bfloat16
MEM = 8
LANES = 128
WIDE = 4


def split(x):
    hi = x.astype(BF16)
    lo = (x - hi.astype(F32)).astype(BF16)
    return hi, lo


def dot(a, b):
    return jnp.dot(a, b, preferred_element_type=F32)


def dot_nt(a, b):
    return lax.dot_general(a, b, (((1,), (1,)), ((), ())), preferred_element_type=F32)


def mul3(a, b):
    (ah, al), (bh, bl) = a, b
    return dot(ah, bh) + (dot(ah, bl) + dot(al, bh))


def exchange_lanes(parts, first, second):
    out = list(parts)
    for bit, shift, odd in ((1, 32, first), (2, 64, second)):
        for low in range(4):
            if low & bit:
                continue
            a, b = out[low], out[low | bit]
            out[low] = jnp.where(odd, pltpu.roll(b, shift, 1), a)
            out[low | bit] = jnp.where(odd, b, pltpu.roll(a, LANES - shift, 1))
    return out


def lane_bits(rows):
    lane = lax.broadcasted_iota(jnp.int32, (rows, LANES), 1)
    return (lane // 32) % 2 == 1, lane // 64 == 1


def obs_kernel(where_ref, prior_ref, map_ref, extra_ref, *refs):
    pieces, obs_ref, stack = refs[:MEM], refs[MEM], refs[MEM + 1]
    members = prior_ref.shape[0]
    me = where_ref[0]
    first, second = lane_bits(members)
    for s in range(MEM):
        peer = me ^ s
        for c in range(4):
            base = pl.multiple_of(peer * 512 + c * LANES, LANES)
            layers = [prior_ref[:, l, pl.ds(base, LANES)] for l in range(4)]
            groups = exchange_lanes(layers, first, second)
            for g in range(4):
                at = c * 4 + g
                pieces[s][:, at * LANES : (at + 1) * LANES] = groups[g]
                row = pl.multiple_of((peer * 2 + at // 8) * members, members)
                stack[pl.ds(row, members), (at % 8) * LANES : (at % 8 + 1) * LANES] = groups[g]
    halves = [map_ref[l, 32 * h : 32 * h + 32, :] for h in range(2) for l in range(4)]
    tall = jnp.concatenate(halves, axis=0)
    wide = jnp.concatenate([tall] * 4, axis=1)
    big = jnp.concatenate([wide] * 4, axis=0)
    row = lax.broadcasted_iota(jnp.int32, big.shape, 0)
    lane = lax.broadcasted_iota(jnp.int32, big.shape, 1)
    weights = jnp.where(row // 256 == lane // 32, big, 0.0)
    values = mul3(split(stack[...]), split(weights))
    for q in range(16):
        obs_ref[:, q * LANES : (q + 1) * LANES] = values[q * members : (q + 1) * members]
    obs_ref[0:8, 2048:2176] = extra_ref[...]
    obs_ref[8:, 2048:2176] = jnp.zeros((members - 8, LANES), F32)


def local_obs(where, prior, measurement_matrix, extra):
    members = prior.shape[0]
    vmem = pl.BlockSpec(memory_space=pltpu.VMEM)
    return pl.pallas_call(
        obs_kernel,
        out_shape=[jax.ShapeDtypeStruct((members, 2048), F32)] * MEM
        + [jax.ShapeDtypeStruct((members, 2176), F32)],
        in_specs=[pl.BlockSpec(memory_space=pltpu.SMEM), vmem, vmem, vmem],
        out_specs=[vmem] * (MEM + 1),
        scratch_shapes=[pltpu.VMEM((512, 1024), F32)],
        compiler_params=pltpu.CompilerParams(vmem_limit_bytes=48 << 20),
        name="local_obs",
    )(where, prior, measurement_matrix, extra)


def square(p):
    h, l = p
    m = dot(h, l)
    return dot(h, h) + (m + dot(l, h))


def each(function, *lists):
    return [function(*items) for items in zip(*lists)]


def mixing_kernel(*refs):
    where_ref, column_ref, weight_ref = refs[:3]
    obs = refs[3:18]
    root_ref, offset_ref, raw, table, sems = refs[18:]
    me = where_ref[0]

    @pl.when(pl.program_id(0) == 0)
    def gather():
        copies = [[], [], []]

        def place(source, row, slot, peer):
            copies[slot].append(
                pltpu.make_async_copy(
                    source.at[pl.ds(row, 32), :],
                    raw.at[slot, pl.ds(pl.multiple_of(peer * 32, 32), 32), :],
                    sems.at[slot, len(copies[slot])],
                )
            )

        for slot, (own, one, three, two_own, two_far) in zip((0, 2, 1), (obs[:5], obs[5:10], obs[10:])):
            for source, x in ((own, 0), (one, 1), (three, 3)):
                for y in range(2):
                    place(source, y * 32, slot, me ^ x ^ (4 * y))
            place(two_own, 0, slot, me ^ 2)
            place(two_far, 0, slot, me ^ 6)
        for slot in range(3):
            for copy in copies[slot]:
                copy.start()
        for slot in range(3):
            for copy in copies[slot]:
                copy.wait()
            extras = [raw[slot, 32 * m : 32 * m + 8, 2048:2176] for m in range(MEM)]
            reading = jnp.concatenate([e[i : i + 1] for e in extras for i in (0, 1)], axis=1)
            spread = jnp.concatenate([e[i : i + 1] for e in extras for i in (2, 3)], axis=1)
            scale = 1.0 / jnp.sqrt(spread)
            for c in range(16):
                lanes = slice(c * LANES, (c + 1) * LANES)
                value = raw[slot, :, lanes]
                mean = jnp.sum(value, axis=0, keepdims=True) * (1.0 / 256.0)
                table[slot * 16 + c, 0:256, :] = (value - mean) * scale[:, lanes]
                table[slot * 16 + c, 256:264, :] = jnp.broadcast_to(
                    (reading[:, lanes] - mean) * scale[:, lanes], (8, LANES)
                )
        offset_ref[...] = jnp.zeros((256, LANES), F32)

    rows = lax.broadcasted_iota(jnp.int32, (256, 256), 0)
    cols = lax.broadcasted_iota(jnp.int32, (256, 256), 1)
    diagonal = rows == cols
    block = lax.broadcasted_iota(jnp.int32, (1, LANES), 1) // 32
    lane = lax.broadcasted_iota(jnp.int32, (256, LANES), 1)

    def pick(g):
        halves = []
        for h in range(2):
            piece = jnp.zeros((264, LANES), F32)
            factor = jnp.zeros((1, LANES), F32)
            for i in range(4):
                place_at = column_ref[g * 8 + 4 * h + i]
                shift = lax.rem(i - lax.rem(place_at, 4) + 4, 4) * 32
                moved = pltpu.roll(table[place_at // 4], shift, 1)
                piece = jnp.where(block == i, moved, piece)
                factor = jnp.where(block == i, weight_ref[g * 8 + 4 * h + i], factor)
            halves.append(piece * factor)
        return jnp.concatenate(halves, axis=1)

    groups = [pl.program_id(0) * WIDE + u for u in range(WIDE)]
    picked = each(pick, groups)
    drives = each(
        lambda p: jnp.sum(p[0:256] * p[256:257], axis=1, keepdims=True), picked
    )
    parts = each(lambda p: split(p[0:256]), picked)
    grams = each(
        lambda p: dot_nt(p[0], p[0]) + (dot_nt(p[0], p[1]) + dot_nt(p[1], p[0])), parts
    )
    grams = each(lambda g: g + jnp.where(diagonal, 255.0, 0.0), grams)
    inverses = each(
        lambda g: 1.0
        / jnp.max(jnp.sum(jnp.abs(g), axis=0, keepdims=True), axis=1, keepdims=True),
        grams,
    )
    current = each(lambda g, v: g * v, grams, inverses)
    roots = []
    for step in range(3):
        parts = each(split, current)
        second = each(square, parts)
        if step < 2:
            products = each(mul3, parts, each(split, second))
        if step != 1:
            mixed = each(lambda s, c: split(s - 4.5 * c), second, current)
            roots.append(
                each(
                    lambda m, s, c: 0.0625 * square(m)
                    + (0.421875 * s - 2.4375 * c + jnp.where(diagonal, 2.25, 0.0)),
                    mixed,
                    second,
                    current,
                )
            )
        if step < 2:
            current = each(
                lambda c, s, p: 2.25 * c - 1.5 * s + 0.25 * p, current, second, products
            )
    root = each(mul3, each(split, roots[0]), each(split, roots[1]))
    inner = each(lambda r, d: jnp.sum(r * d, axis=0, keepdims=True), root, drives)
    offsets = each(
        lambda r, n, v: jnp.sum(r * n, axis=1, keepdims=True) * v, root, inner, inverses
    )
    held = offset_ref[...]
    for u, (g, r, v, o) in enumerate(zip(groups, root, inverses, offsets)):
        root_ref[u] = jnp.sqrt(255.0 * v) * r
        held = jnp.where(lane == g, o, held)
    offset_ref[...] = held


def apply_kernel(where_ref, root_ref, offset_ref, *refs):
    pieces = refs[:MEM]
    out_ref, field = refs[MEM:]
    me = where_ref[0]

    @pl.when(pl.program_id(0) == 0)
    def gather():
        for s in range(MEM):
            row = pl.multiple_of((me ^ s) * 32, 32)
            for g in range(16):
                field[g, pl.ds(row, 32), :] = pieces[s][:, g * LANES : (g + 1) * LANES]

    odd, high = lane_bits(256)
    lane = lax.broadcasted_iota(jnp.int32, (256, LANES), 1)
    groups = [pl.program_id(0) * 4 + g for g in range(4)]
    value = [field[g] for g in groups]
    centre = each(lambda x: jnp.sum(x, axis=0, keepdims=True) * (1.0 / 256.0), value)
    anomaly = each(lambda x, a: x - a, value, centre)
    offset = [
        jnp.sum(jnp.where(lane == g, offset_ref[...], 0.0), axis=1, keepdims=True) for g in groups
    ]
    base = each(
        lambda a, x, o: a + jnp.sum(x * o, axis=0, keepdims=True), centre, anomaly, offset
    )
    spread = each(mul3, [split(root_ref[u]) for u in range(4)], each(split, anomaly))
    layers = exchange_lanes(each(lambda b, x: b + x, base, spread), odd, high)
    for l in range(4):
        out_ref[:, l, :] = layers[l]


VMEM = pl.BlockSpec(memory_space=pltpu.VMEM)
SMEM = pl.BlockSpec(memory_space=pltpu.SMEM)
ANYWHERE = pl.BlockSpec(memory_space=pl.ANY)


def find_mixing(where, columns, weights, obs):
    return pl.pallas_call(
        mixing_kernel,
        out_shape=[
            jax.ShapeDtypeStruct((16, 256, 256), F32),
            jax.ShapeDtypeStruct((256, LANES), F32),
        ],
        grid=(16 // WIDE,),
        in_specs=[SMEM] * 3 + [ANYWHERE] * 15,
        out_specs=[
            pl.BlockSpec((WIDE, 256, 256), lambda i: (i, 0, 0)),
            pl.BlockSpec((256, LANES), lambda i: (0, 0)),
        ],
        scratch_shapes=[
            pltpu.VMEM((3, 256, 2176), F32),
            pltpu.VMEM((48, 264, LANES), F32),
            pltpu.SemaphoreType.DMA((3, 8)),
        ],
        compiler_params=pltpu.CompilerParams(vmem_limit_bytes=48 << 20),
        cost_estimate=pl.CostEstimate(
            flops=16 * 30 * 2 * 256**3, bytes_accessed=12 << 20, transcendentals=0
        ),
        name="mixing",
    )(where, columns, weights, *obs)


def apply_mixing(where, root, offset, pieces):
    return pl.pallas_call(
        apply_kernel,
        out_shape=jax.ShapeDtypeStruct((256, 4, 512), F32),
        grid=(4,),
        in_specs=[SMEM, pl.BlockSpec((4, 256, 256), lambda i: (i, 0, 0)), VMEM] + [VMEM] * MEM,
        out_specs=pl.BlockSpec((256, 4, LANES), lambda i: (0, 0, i)),
        scratch_shapes=[pltpu.VMEM((16, 256, LANES), F32)],
        compiler_params=pltpu.CompilerParams(vmem_limit_bytes=60 << 20),
        name="apply",
    )(where, root, offset, *pieces)


def send(x, flip):
    return lax.ppermute(x, "mem", [(i, i ^ flip) for i in range(MEM)])


def swap_cores(x):
    return lax.ppermute(x, "tile", [(i, i ^ 1) for i in range(32)])


def local(prior, measurement_matrix, readings, noise, nearby, damping):
    me = lax.axis_index("mem").astype(jnp.int32)
    tile = lax.axis_index("tile").astype(jnp.int32)
    where = jnp.stack([me, tile])
    extra = jnp.concatenate(
        [readings.reshape(2, 128), noise.reshape(2, 128), jnp.zeros((4, 128), F32)], axis=0
    )
    *pieces, obs = local_obs(where, prior, measurement_matrix, extra)
    outer = lax.ppermute(
        obs,
        "tile",
        [(i, i + 1) for i in range(1, 31, 2)] + [(i + 1, i) for i in range(1, 31, 2)],
    )
    own = jnp.concatenate([obs, send(obs, 4)], axis=0)
    got = [pieces[0]] + [send(pieces[s], s) for s in range(1, 4)]
    own1, own3 = send(own, 1), send(own, 3)
    far = jnp.concatenate([outer, send(outer, 4)], axis=0)
    far1, far3 = send(far, 1), send(far, 3)
    own2 = [send(own3[:32], 1), send(own1[32:], 3)]
    sib = [swap_cores(x) for x in (own, own1, own3, *own2)]
    far2 = [send(far3[:32], 1), send(far1[32:], 3)]
    *late, _ = lax.optimization_barrier((*pieces[4:], far1))
    got += [send(x, s) for s, x in zip(range(4, MEM), late)]
    obs = (own, own1, own3, *own2, far, far1, far3, *far2, *sib)
    block_tile = nearby // 64
    slot = jnp.where(block_tile == tile, 0, jnp.where(block_tile // 2 == tile // 2, 1, 2))
    columns = (slot * 64 + nearby % 64).reshape(-1)
    weights = jnp.sqrt(1.0 / (1.0 + damping.astype(F32))).reshape(-1)
    root, offset = find_mixing(
        where, columns, weights, obs
    )
    return apply_mixing(where, root, offset, got)


def solution(mesh):
    in_specs = (
        P("mem", None, "tile"),
        P(),
        P(("tile", "mem"), None),
        P(("tile", "mem"), None),
        P(("tile", "mem"), None),
        P(("tile", "mem"), None),
    )
    out_specs = P(None, None, ("tile", "mem"))
    return jax.shard_map(local, mesh=mesh, in_specs=in_specs, out_specs=out_specs, check_vma=False)
```

```python
import jax
import jax.numpy as jnp
from jax import lax
from jax.experimental import pallas as pl
from jax.experimental.pallas import tpu as pltpu
from jax.sharding import PartitionSpec as P

F32 = jnp.float32
BF16 = jnp.bfloat16
MEM = 8
LANES = 128
WIDE = 4


def split(x):
    hi = x.astype(BF16)
    lo = (x - hi.astype(F32)).astype(BF16)
    return hi, lo


def dot(a, b):
    return jnp.dot(a, b, preferred_element_type=F32)


def dot_nt(a, b):
    return lax.dot_general(a, b, (((1,), (1,)), ((), ())), preferred_element_type=F32)


def mul3(a, b):
    (ah, al), (bh, bl) = a, b
    return dot(ah, bh) + (dot(ah, bl) + dot(al, bh))


def exchange_lanes(parts, first, second):
    out = list(parts)
    for bit, shift, odd in ((1, 32, first), (2, 64, second)):
        for low in range(4):
            if low & bit:
                continue
            a, b = out[low], out[low | bit]
            out[low] = jnp.where(odd, pltpu.roll(b, shift, 1), a)
            out[low | bit] = jnp.where(odd, b, pltpu.roll(a, LANES - shift, 1))
    return out


def lane_bits(rows):
    lane = lax.broadcasted_iota(jnp.int32, (rows, LANES), 1)
    return (lane // 32) % 2 == 1, lane // 64 == 1


def obs_kernel(where_ref, prior_ref, map_ref, reading_ref, noise_ref, *refs):
    pieces, obs_ref, stack = refs[:MEM], refs[MEM], refs[MEM + 1]
    members = prior_ref.shape[0]
    me = where_ref[0]
    first, second = lane_bits(members)
    for s in range(MEM):
        peer = me ^ s
        for c in range(4):
            base = pl.multiple_of(peer * 512 + c * LANES, LANES)
            layers = [prior_ref[:, l, pl.ds(base, LANES)] for l in range(4)]
            groups = exchange_lanes(layers, first, second)
            for g in range(4):
                at = c * 4 + g
                pieces[s][:, at * LANES : (at + 1) * LANES] = groups[g]
                row = pl.multiple_of((peer * 2 + at // 8) * members, members)
                stack[pl.ds(row, members), (at % 8) * LANES : (at % 8 + 1) * LANES] = groups[g]
    halves = [map_ref[l, :, 32 * h : 32 * h + 32] for h in range(2) for l in range(4)]
    thin = jnp.concatenate(halves, axis=1)
    tall = jnp.concatenate([thin] * 4, axis=0)
    big = jnp.concatenate([tall] * 4, axis=1)
    row = lax.broadcasted_iota(jnp.int32, big.shape, 0)
    lane = lax.broadcasted_iota(jnp.int32, big.shape, 1)
    weights = jnp.where(lane // 256 == row // 32, big, 0.0)
    (xh, xl), (wh, wl) = split(stack[...]), split(weights)
    values = dot_nt(xh, wh) + (dot_nt(xh, wl) + dot_nt(xl, wh))
    for q in range(16):
        obs_ref[:, q * LANES : (q + 1) * LANES] = values[q * members : (q + 1) * members]
    obs_ref[:, 2048:2176] = jnp.zeros((members, LANES), F32)
    for at, ref in enumerate((reading_ref, noise_ref)):
        for half in range(2):
            line = [ref[half * 4 + j : half * 4 + j + 1, :] for j in range(4)]
            at_row = at * 2 + half
            obs_ref[at_row : at_row + 1, 2048:2176] = jnp.concatenate(line, axis=1)


def local_obs(where, prior, measurement_map, readings, noise):
    members = prior.shape[0]
    vmem = pl.BlockSpec(memory_space=pltpu.VMEM)
    return pl.pallas_call(
        obs_kernel,
        out_shape=[jax.ShapeDtypeStruct((members, 2048), F32)] * MEM
        + [jax.ShapeDtypeStruct((members, 2176), F32)],
        in_specs=[pl.BlockSpec(memory_space=pltpu.SMEM)] + [vmem] * 4,
        out_specs=[vmem] * (MEM + 1),
        scratch_shapes=[pltpu.VMEM((512, 1024), F32)],
        compiler_params=pltpu.CompilerParams(vmem_limit_bytes=24 << 20),
        name="local_obs",
    )(where, prior, measurement_map, readings, noise)


def square(p):
    h, l = p
    m = dot(h, l)
    return dot(h, h) + (m + dot(l, h))


def each(function, *lists):
    return [function(*items) for items in zip(*lists)]


def mixing_kernel(*refs):
    where_ref, column_ref, weight_ref = refs[:3]
    obs = refs[3:18]
    root_ref, offset_ref, raw, table, sems = refs[18:]
    me = where_ref[0]

    @pl.when(pl.program_id(0) == 0)
    def gather():
        copies = [[], [], []]

        def place(source, row, slot, peer):
            copies[slot].append(
                pltpu.make_async_copy(
                    source.at[pl.ds(row, 32), :],
                    raw.at[slot, pl.ds(pl.multiple_of(peer * 32, 32), 32), :],
                    sems.at[slot, len(copies[slot])],
                )
            )

        for slot, (own, one, three, two_own, two_far) in zip((0, 2, 1), (obs[:5], obs[5:10], obs[10:])):
            for source, x in ((own, 0), (one, 1), (three, 3)):
                for y in range(2):
                    place(source, y * 32, slot, me ^ x ^ (4 * y))
            place(two_own, 0, slot, me ^ 2)
            place(two_far, 0, slot, me ^ 6)
        for slot in range(3):
            for copy in copies[slot]:
                copy.start()
        for slot in range(3):
            for copy in copies[slot]:
                copy.wait()
            extras = [raw[slot, 32 * m : 32 * m + 8, 2048:2176] for m in range(MEM)]
            reading = jnp.concatenate([e[i : i + 1] for e in extras for i in (0, 1)], axis=1)
            spread = jnp.concatenate([e[i : i + 1] for e in extras for i in (2, 3)], axis=1)
            scale = 1.0 / jnp.sqrt(spread)
            for c in range(16):
                lanes = slice(c * LANES, (c + 1) * LANES)
                value = raw[slot, :, lanes]
                mean = jnp.sum(value, axis=0, keepdims=True) * (1.0 / 256.0)
                table[slot * 16 + c, 0:256, :] = (value - mean) * scale[:, lanes]
                table[slot * 16 + c, 256:264, :] = jnp.broadcast_to(
                    (reading[:, lanes] - mean) * scale[:, lanes], (8, LANES)
                )
        offset_ref[...] = jnp.zeros((256, LANES), F32)

    rows = lax.broadcasted_iota(jnp.int32, (256, 256), 0)
    cols = lax.broadcasted_iota(jnp.int32, (256, 256), 1)
    diagonal = rows == cols
    block = lax.broadcasted_iota(jnp.int32, (1, LANES), 1) // 32
    lane = lax.broadcasted_iota(jnp.int32, (256, LANES), 1)

    def pick(g):
        halves = []
        for h in range(2):
            piece = jnp.zeros((264, LANES), F32)
            factor = jnp.zeros((1, LANES), F32)
            for i in range(4):
                place_at = column_ref[g * 8 + 4 * h + i]
                shift = lax.rem(i - lax.rem(place_at, 4) + 4, 4) * 32
                moved = pltpu.roll(table[place_at // 4], shift, 1)
                piece = jnp.where(block == i, moved, piece)
                factor = jnp.where(block == i, weight_ref[g * 8 + 4 * h + i], factor)
            halves.append(piece * factor)
        return jnp.concatenate(halves, axis=1)

    groups = [pl.program_id(0) * WIDE + u for u in range(WIDE)]
    picked = each(pick, groups)
    drives = each(
        lambda p: jnp.sum(p[0:256] * p[256:257], axis=1, keepdims=True), picked
    )
    parts = each(lambda p: split(p[0:256]), picked)
    grams = each(
        lambda p: dot_nt(p[0], p[0]) + (dot_nt(p[0], p[1]) + dot_nt(p[1], p[0])), parts
    )
    grams = each(lambda g: g + jnp.where(diagonal, 255.0, 0.0), grams)
    inverses = each(
        lambda g: 1.0
        / jnp.max(jnp.sum(jnp.abs(g), axis=0, keepdims=True), axis=1, keepdims=True),
        grams,
    )
    current = each(lambda g, v: g * v, grams, inverses)
    roots = []
    for step in range(3):
        parts = each(split, current)
        second = each(square, parts)
        if step < 2:
            products = each(mul3, parts, each(split, second))
        if step != 1:
            mixed = each(lambda s, c: split(s - 4.5 * c), second, current)
            roots.append(
                each(
                    lambda m, s, c: 0.0625 * square(m)
                    + (0.421875 * s - 2.4375 * c + jnp.where(diagonal, 2.25, 0.0)),
                    mixed,
                    second,
                    current,
                )
            )
        if step < 2:
            current = each(
                lambda c, s, p: 2.25 * c - 1.5 * s + 0.25 * p, current, second, products
            )
    root = each(mul3, each(split, roots[0]), each(split, roots[1]))
    inner = each(lambda r, d: jnp.sum(r * d, axis=0, keepdims=True), root, drives)
    offsets = each(
        lambda r, n, v: jnp.sum(r * n, axis=1, keepdims=True) * v, root, inner, inverses
    )
    held = offset_ref[...]
    for u, (g, r, v, o) in enumerate(zip(groups, root, inverses, offsets)):
        root_ref[u] = jnp.sqrt(255.0 * v) * r
        held = jnp.where(lane == g, o, held)
    offset_ref[...] = held


def apply_kernel(where_ref, root_ref, offset_ref, *refs):
    pieces = refs[:MEM]
    out_ref, field = refs[MEM:]
    me = where_ref[0]

    @pl.when(pl.program_id(0) == 0)
    def gather():
        for s in range(MEM):
            row = pl.multiple_of((me ^ s) * 32, 32)
            for g in range(16):
                field[g, pl.ds(row, 32), :] = pieces[s][:, g * LANES : (g + 1) * LANES]

    odd, high = lane_bits(256)
    lane = lax.broadcasted_iota(jnp.int32, (256, LANES), 1)
    groups = [pl.program_id(0) * 4 + g for g in range(4)]
    value = [field[g] for g in groups]
    centre = each(lambda x: jnp.sum(x, axis=0, keepdims=True) * (1.0 / 256.0), value)
    anomaly = each(lambda x, a: x - a, value, centre)
    offset = [
        jnp.sum(jnp.where(lane == g, offset_ref[...], 0.0), axis=1, keepdims=True) for g in groups
    ]
    base = each(
        lambda a, x, o: a + jnp.sum(x * o, axis=0, keepdims=True), centre, anomaly, offset
    )
    spread = each(mul3, [split(root_ref[u]) for u in range(4)], each(split, anomaly))
    layers = exchange_lanes(each(lambda b, x: b + x, base, spread), odd, high)
    for l in range(4):
        out_ref[:, l, :] = layers[l]


VMEM = pl.BlockSpec(memory_space=pltpu.VMEM)
SMEM = pl.BlockSpec(memory_space=pltpu.SMEM)
ANYWHERE = pl.BlockSpec(memory_space=pl.ANY)


def find_mixing(where, columns, weights, obs):
    return pl.pallas_call(
        mixing_kernel,
        out_shape=[
            jax.ShapeDtypeStruct((16, 256, 256), F32),
            jax.ShapeDtypeStruct((256, LANES), F32),
        ],
        grid=(16 // WIDE,),
        in_specs=[SMEM] * 3 + [ANYWHERE] * 15,
        out_specs=[
            pl.BlockSpec((WIDE, 256, 256), lambda i: (i, 0, 0)),
            pl.BlockSpec((256, LANES), lambda i: (0, 0)),
        ],
        scratch_shapes=[
            pltpu.VMEM((3, 256, 2176), F32),
            pltpu.VMEM((48, 264, LANES), F32),
            pltpu.SemaphoreType.DMA((3, 8)),
        ],
        compiler_params=pltpu.CompilerParams(vmem_limit_bytes=30 << 20),
        cost_estimate=pl.CostEstimate(
            flops=16 * 30 * 2 * 256**3, bytes_accessed=12 << 20, transcendentals=0
        ),
        name="mixing",
    )(where, columns, weights, *obs)


def apply_mixing(where, root, offset, pieces):
    return pl.pallas_call(
        apply_kernel,
        out_shape=jax.ShapeDtypeStruct((256, 4, 512), F32),
        grid=(4,),
        in_specs=[SMEM, pl.BlockSpec((4, 256, 256), lambda i: (i, 0, 0)), VMEM] + [VMEM] * MEM,
        out_specs=pl.BlockSpec((256, 4, LANES), lambda i: (0, 0, i)),
        scratch_shapes=[pltpu.VMEM((16, 256, LANES), F32)],
        compiler_params=pltpu.CompilerParams(vmem_limit_bytes=24 << 20),
        name="apply",
    )(where, root, offset, *pieces)


def send(x, flip):
    return lax.ppermute(x, "mem", [(i, i ^ flip) for i in range(MEM)])


def swap_cores(x):
    return lax.ppermute(x, "tile", [(i, i ^ 1) for i in range(32)])


def local(prior, measurement_matrix, readings, noise, nearby, damping):
    me = lax.axis_index("mem").astype(jnp.int32)
    tile = lax.axis_index("tile").astype(jnp.int32)
    where = jnp.stack([me, tile])
    measurement_map = jnp.swapaxes(measurement_matrix, 1, 2)
    *pieces, obs = local_obs(where, prior, measurement_map, readings, noise)
    hold = lax.optimization_barrier
    across, got1, got3 = send(obs, 4), send(pieces[1], 1), send(pieces[3], 3)
    across, got1, got3, obs = hold((across, got1, got3, obs))
    own = jnp.concatenate([obs, across], axis=0)
    own1, own3 = send(own, 1), send(own, 3)
    outer = lax.ppermute(
        obs,
        "tile",
        [(i, i + 1) for i in range(1, 31, 2)] + [(i + 1, i) for i in range(1, 31, 2)],
    )
    own1, own3, outer = hold((own1, own3, outer))
    own2 = [send(own3[:32], 1), send(own1[32:], 3)]
    far = jnp.concatenate([outer, send(outer, 4)], axis=0)
    sib = [swap_cores(x) for x in (own, own1, own3)]
    far, *rest = hold((far, *own2, *sib))
    own2, sib = rest[:2], rest[2:]
    far1, far3 = send(far, 1), send(far, 3)
    sib += [swap_cores(x) for x in own2]
    far1, far3, *rest = hold((far1, far3, *pieces[4:], pieces[2]))
    far2 = [send(far3[:32], 1), send(far1[32:], 3)]
    late = [send(x, s) for s, x in zip((4, 5, 6, 7, 2), rest)]
    got = [pieces[0], got1, late[4], got3, *late[:4]]
    obs = (own, own1, own3, *own2, far, far1, far3, *far2, *sib)
    block_tile = nearby // 64
    slot = jnp.where(block_tile == tile, 0, jnp.where(block_tile // 2 == tile // 2, 1, 2))
    columns = (slot * 64 + nearby % 64).reshape(-1)
    weights = jnp.sqrt(1.0 / (1.0 + damping.astype(F32))).reshape(-1)
    root, offset = find_mixing(
        where, columns, weights, obs
    )
    return apply_mixing(where, root, offset, got)


def solution(mesh):
    in_specs = (
        P("mem", None, "tile"),
        P(),
        P(("tile", "mem"), None),
        P(("tile", "mem"), None),
        P(("tile", "mem"), None),
        P(("tile", "mem"), None),
    )
    out_specs = P(None, None, ("tile", "mem"))
    return jax.shard_map(local, mesh=mesh, in_specs=in_specs, out_specs=out_specs, check_vma=False)
```

```python
import jax
import jax.numpy as jnp
from jax import lax
from jax.experimental import pallas as pl
from jax.experimental.pallas import tpu as pltpu
from jax.sharding import PartitionSpec as P

F32 = jnp.float32
BF16 = jnp.bfloat16
MEM = 8
LANES = 128
WIDE = 4
LIMIT = 62 << 20
VMEM = pl.BlockSpec(memory_space=pltpu.VMEM)
SMEM = pl.BlockSpec(memory_space=pltpu.SMEM)
ANYWHERE = pl.BlockSpec(memory_space=pl.ANY)
HBM = pl.BlockSpec(memory_space=pltpu.HBM)


def split(x):
    hi = x.astype(BF16)
    lo = (x - hi.astype(F32)).astype(BF16)
    return hi, lo


def dot(a, b):
    return jnp.dot(a, b, preferred_element_type=F32)


def dot_nt(a, b):
    return lax.dot_general(a, b, (((1,), (1,)), ((), ())), preferred_element_type=F32)


def mul3(a, b):
    (ah, al), (bh, bl) = a, b
    return dot(ah, bh) + (dot(ah, bl) + dot(al, bh))


def exchange_lanes(parts, first, second):
    out = list(parts)
    for bit, shift, odd in ((1, 32, first), (2, 64, second)):
        for low in range(4):
            if low & bit:
                continue
            a, b = out[low], out[low | bit]
            out[low] = jnp.where(odd, pltpu.roll(b, shift, 1), a)
            out[low | bit] = jnp.where(odd, b, pltpu.roll(a, LANES - shift, 1))
    return out


def lane_bits(rows):
    lane = lax.broadcasted_iota(jnp.int32, (rows, LANES), 1)
    return (lane // 32) % 2 == 1, lane // 64 == 1


def obs_kernel(where_ref, prior_ref, map_ref, reading_ref, noise_ref, *refs):
    pieces, obs_ref = refs[:MEM], refs[MEM]
    part, staged, stack, map_in, reading_in, noise_in, in_sems, out_sems = refs[MEM + 1 :]
    members = prior_ref.shape[0]
    me = where_ref[0]
    reads = []
    for s in range(MEM):
        cells = pl.ds(pl.multiple_of((me ^ s) * 512, 512), 512)
        reads.append(pltpu.make_async_copy(prior_ref.at[:, :, cells], part.at[s], in_sems.at[s]))
    for at, (source, target) in enumerate(
        ((map_ref, map_in), (reading_ref, reading_in), (noise_ref, noise_in))
    ):
        reads.append(pltpu.make_async_copy(source, target, in_sems.at[MEM + at]))
    writes = [
        pltpu.make_async_copy(staged.at[s], pieces[s], out_sems.at[s]) for s in range(MEM)
    ]
    for read in reads:
        read.start()
    first, second = lane_bits(members)
    for s in range(MEM):
        peer = me ^ s
        reads[s].wait()
        for c in range(4):
            lanes = slice(c * LANES, (c + 1) * LANES)
            layers = [part[s, :, l, lanes] for l in range(4)]
            groups = exchange_lanes(layers, first, second)
            for g in range(4):
                at = c * 4 + g
                staged[s, :, at * LANES : (at + 1) * LANES] = groups[g]
                row = pl.multiple_of((peer * 2 + at // 8) * members, members)
                stack[pl.ds(row, members), (at % 8) * LANES : (at % 8 + 1) * LANES] = groups[g]
        writes[s].start()
    for read in reads[MEM:]:
        read.wait()
    halves = [map_in[l, :, 32 * h : 32 * h + 32] for h in range(2) for l in range(4)]
    thin = jnp.concatenate(halves, axis=1)
    tall = jnp.concatenate([thin] * 4, axis=0)
    big = jnp.concatenate([tall] * 4, axis=1)
    row = lax.broadcasted_iota(jnp.int32, big.shape, 0)
    lane = lax.broadcasted_iota(jnp.int32, big.shape, 1)
    weights = jnp.where(lane // 256 == row // 32, big, 0.0)
    (xh, xl), (wh, wl) = split(stack[...]), split(weights)
    values = dot_nt(xh, wh) + (dot_nt(xh, wl) + dot_nt(xl, wh))
    for q in range(16):
        obs_ref[:, q * LANES : (q + 1) * LANES] = values[q * members : (q + 1) * members]
    obs_ref[:, 2048:2176] = jnp.zeros((members, LANES), F32)
    for at, ref in enumerate((reading_in, noise_in)):
        for half in range(2):
            line = [ref[half * 4 + j : half * 4 + j + 1, :] for j in range(4)]
            at_row = at * 2 + half
            obs_ref[at_row : at_row + 1, 2048:2176] = jnp.concatenate(line, axis=1)
    for write in writes:
        write.wait()


def local_obs(where, prior, measurement_map, readings, noise):
    members = prior.shape[0]
    return pl.pallas_call(
        obs_kernel,
        out_shape=[jax.ShapeDtypeStruct((members, 2048), F32)] * MEM
        + [jax.ShapeDtypeStruct((members, 2176), F32)],
        in_specs=[SMEM] + [HBM] * 4,
        out_specs=[HBM] * MEM + [VMEM],
        scratch_shapes=[
            pltpu.VMEM((MEM, members, 4, 512), F32),
            pltpu.VMEM((MEM, members, 2048), F32),
            pltpu.VMEM((512, 1024), F32),
            pltpu.VMEM(measurement_map.shape, F32),
            pltpu.VMEM(readings.shape, F32),
            pltpu.VMEM(noise.shape, F32),
            pltpu.SemaphoreType.DMA((MEM + 3,)),
            pltpu.SemaphoreType.DMA((MEM,)),
        ],
        compiler_params=pltpu.CompilerParams(vmem_limit_bytes=LIMIT),
        name="local_obs",
    )(where, prior, measurement_map, readings, noise)


def square(p):
    h, l = p
    m = dot(h, l)
    return dot(h, h) + (m + dot(l, h))


def each(function, *lists):
    return [function(*items) for items in zip(*lists)]


PLACES = (0, 4, 1, 3, 5, 7, 2, 6)


def placing(me, sources, raw, sems):
    return [
        pltpu.make_async_copy(
            source, raw.at[pl.ds(pl.multiple_of((me ^ x) * 32, 32), 32), :], sems.at[at]
        )
        for at, (x, source) in enumerate(zip(PLACES, sources))
    ]


def scale_tile(raw, table, first):
    extras = [raw[32 * m : 32 * m + 8, 2048:2176] for m in range(MEM)]
    reading = jnp.concatenate([e[i : i + 1] for e in extras for i in (0, 1)], axis=1)
    noise = jnp.concatenate([e[i : i + 1] for e in extras for i in (2, 3)], axis=1)
    scale = 1.0 / jnp.sqrt(noise)
    for c in range(16):
        lanes = slice(c * LANES, (c + 1) * LANES)
        value = raw[:, lanes]
        mean = jnp.sum(value, axis=0, keepdims=True) * (1.0 / 256.0)
        table[first + c, 0:256, :] = (value - mean) * scale[:, lanes]
        table[first + c, 256:264, :] = jnp.broadcast_to(
            (reading[:, lanes] - mean) * scale[:, lanes], (8, LANES)
        )


def table_kernel(where_ref, *refs):
    table_ref, raw, sems = refs[MEM:]
    copies = placing(where_ref[0], refs[:MEM], raw, sems)
    for copy in copies:
        copy.start()
    for copy in copies:
        copy.wait()
    scale_tile(raw, table_ref, 0)


def own_table(where, parts):
    return pl.pallas_call(
        table_kernel,
        out_shape=jax.ShapeDtypeStruct((16, 264, LANES), F32),
        in_specs=[SMEM] + [ANYWHERE] * MEM,
        out_specs=VMEM,
        scratch_shapes=[pltpu.VMEM((256, 2176), F32), pltpu.SemaphoreType.DMA((MEM,))],
        compiler_params=pltpu.CompilerParams(vmem_limit_bytes=12 << 20),
        cost_estimate=pl.CostEstimate(
            flops=4 * 256 * 2048, bytes_accessed=6 << 20, transcendentals=2048
        ),
        name="own_table",
    )(where, *parts)


def mixing_kernel(*refs):
    where_ref, near_ref, damp_ref, own_ref, sib_ref = refs[:5]
    far = refs[5 : 5 + MEM]
    root_ref, offset_ref, raw, table, sems = refs[5 + MEM :]

    @pl.when(pl.program_id(0) == 0)
    def gather():
        copies = placing(where_ref[0], far, raw, sems)
        for at, source in enumerate((own_ref, sib_ref)):
            copies.append(
                pltpu.make_async_copy(
                    source, table.at[pl.ds(at * 16, 16)], sems.at[MEM + at]
                )
            )
        for copy in copies:
            copy.start()
        for copy in copies[:MEM]:
            copy.wait()
        scale_tile(raw, table, 32)
        offset_ref[...] = jnp.zeros((256, LANES), F32)
        for copy in copies[MEM:]:
            copy.wait()

    rows = lax.broadcasted_iota(jnp.int32, (256, 256), 0)
    cols = lax.broadcasted_iota(jnp.int32, (256, 256), 1)
    diagonal = rows == cols
    block = lax.broadcasted_iota(jnp.int32, (1, LANES), 1) // 32
    lane = lax.broadcasted_iota(jnp.int32, (256, LANES), 1)

    def pick(g):
        halves = []
        for h in range(2):
            piece = jnp.zeros((264, LANES), F32)
            level = jnp.zeros((1, LANES), jnp.int32)
            for i in range(4):
                entry = near_ref[4 * h + i, g]
                tile = lax.shift_right_logical(entry, 6)
                other = jnp.where((tile ^ where_ref[1]) == 1, 16, 32)
                chunk = jnp.where(tile == where_ref[1], 0, other) + (
                    lax.shift_right_logical(entry, 2) & 15
                )
                shift = ((i - entry) & 3) * 32
                moved = pltpu.roll(table[chunk], shift, 1)
                piece = jnp.where(block == i, moved, piece)
                level = jnp.where(block == i, damp_ref[4 * h + i, g], level)
            halves.append(piece * jnp.sqrt(1.0 / (1.0 + level.astype(F32))))
        return jnp.concatenate(halves, axis=1)

    groups = [pl.program_id(0) * WIDE + u for u in range(WIDE)]
    picked = each(pick, groups)
    drives = each(
        lambda p: jnp.sum(p[0:256] * p[256:257], axis=1, keepdims=True), picked
    )
    parts = each(lambda p: split(p[0:256]), picked)
    grams = each(
        lambda p: dot_nt(p[0], p[0]) + (dot_nt(p[0], p[1]) + dot_nt(p[1], p[0])), parts
    )
    grams = each(lambda g: g + jnp.where(diagonal, 255.0, 0.0), grams)
    inverses = each(
        lambda g: 1.0
        / jnp.max(jnp.sum(jnp.abs(g), axis=0, keepdims=True), axis=1, keepdims=True),
        grams,
    )
    current = each(lambda g, v: g * v, grams, inverses)
    roots = []
    for step in range(3):
        parts = each(split, current)
        second = each(square, parts)
        if step < 2:
            products = each(mul3, parts, each(split, second))
        if step != 1:
            mixed = each(lambda s, c: split(s - 4.5 * c), second, current)
            roots.append(
                each(
                    lambda m, s, c: 0.0625 * square(m)
                    + (0.421875 * s - 2.4375 * c + jnp.where(diagonal, 2.25, 0.0)),
                    mixed,
                    second,
                    current,
                )
            )
        if step < 2:
            current = each(
                lambda c, s, p: 2.25 * c - 1.5 * s + 0.25 * p, current, second, products
            )
    root = each(mul3, each(split, roots[0]), each(split, roots[1]))
    inner = each(lambda r, d: jnp.sum(r * d, axis=0, keepdims=True), root, drives)
    offsets = each(
        lambda r, n, v: jnp.sum(r * n, axis=1, keepdims=True) * v, root, inner, inverses
    )
    held = offset_ref[...]
    for u, (g, r, v, o) in enumerate(zip(groups, root, inverses, offsets)):
        root_ref[u] = jnp.sqrt(255.0 * v) * r
        held = jnp.where(lane == g, o, held)
    offset_ref[...] = held


def apply_kernel(where_ref, root_ref, offset_ref, *refs):
    pieces = refs[:MEM]
    out_ref, field, sems = refs[MEM:]
    me = where_ref[0]

    @pl.when(pl.program_id(0) == 0)
    def gather():
        copies = [
            pltpu.make_async_copy(
                pieces[s], field.at[pl.ds(pl.multiple_of((me ^ s) * 32, 32), 32), :], sems.at[s]
            )
            for s in range(MEM)
        ]
        for copy in copies:
            copy.start()
        for copy in copies:
            copy.wait()

    odd, high = lane_bits(256)
    lane = lax.broadcasted_iota(jnp.int32, (256, LANES), 1)
    groups = [pl.program_id(0) * 4 + g for g in range(4)]
    value = [field[:, pl.ds(pl.multiple_of(g * LANES, LANES), LANES)] for g in groups]
    centre = each(lambda x: jnp.sum(x, axis=0, keepdims=True) * (1.0 / 256.0), value)
    anomaly = each(lambda x, a: x - a, value, centre)
    offset = [
        jnp.sum(jnp.where(lane == g, offset_ref[...], 0.0), axis=1, keepdims=True) for g in groups
    ]
    base = each(
        lambda a, x, o: a + jnp.sum(x * o, axis=0, keepdims=True), centre, anomaly, offset
    )
    spread = each(mul3, [split(root_ref[u]) for u in range(4)], each(split, anomaly))
    layers = exchange_lanes(each(lambda b, x: b + x, base, spread), odd, high)
    for l in range(4):
        out_ref[:, l, :] = layers[l]


def find_mixing(where, nearby, damping, own, sib, far):
    return pl.pallas_call(
        mixing_kernel,
        out_shape=[
            jax.ShapeDtypeStruct((16, 256, 256), F32),
            jax.ShapeDtypeStruct((256, LANES), F32),
        ],
        grid=(16 // WIDE,),
        in_specs=[SMEM] * 3 + [ANYWHERE] * (2 + MEM),
        out_specs=[
            pl.BlockSpec((WIDE, 256, 256), lambda i: (i, 0, 0)),
            pl.BlockSpec((256, LANES), lambda i: (0, 0)),
        ],
        scratch_shapes=[
            pltpu.VMEM((256, 2176), F32),
            pltpu.VMEM((48, 264, LANES), F32),
            pltpu.SemaphoreType.DMA((MEM + 2,)),
        ],
        compiler_params=pltpu.CompilerParams(vmem_limit_bytes=30 << 20),
        cost_estimate=pl.CostEstimate(
            flops=16 * 30 * 2 * 256**3, bytes_accessed=12 << 20, transcendentals=0
        ),
        name="mixing",
    )(where, nearby, damping, own, sib, *far)


def apply_mixing(where, root, offset, pieces):
    return pl.pallas_call(
        apply_kernel,
        out_shape=jax.ShapeDtypeStruct((256, 4, 512), F32),
        grid=(4,),
        in_specs=[SMEM, pl.BlockSpec((4, 256, 256), lambda i: (i, 0, 0)), VMEM] + [ANYWHERE] * MEM,
        out_specs=pl.BlockSpec((256, 4, LANES), lambda i: (0, 0, i)),
        scratch_shapes=[pltpu.VMEM((256, 2048), F32), pltpu.SemaphoreType.DMA((MEM,))],
        compiler_params=pltpu.CompilerParams(vmem_limit_bytes=30 << 20),
        name="apply",
    )(where, root, offset, *pieces)


def send(x, flip):
    return lax.ppermute(x, "mem", [(i, i ^ flip) for i in range(MEM)])


def swap_cores(x):
    return lax.ppermute(x, "tile", [(i, i ^ 1) for i in range(32)])


def local(prior, measurement_matrix, readings, noise, nearby, damping):
    me = lax.axis_index("mem").astype(jnp.int32)
    tile = lax.axis_index("tile").astype(jnp.int32)
    where = jnp.stack([me, tile])
    measurement_map = jnp.swapaxes(measurement_matrix, 1, 2)
    *pieces, obs = local_obs(where, prior, measurement_map, readings, noise)
    hold = lax.optimization_barrier
    got = [pieces[0]] + [None] * 7
    own4, own1, own3 = send(obs, 4), send(obs, 1), send(obs, 3)
    far0 = lax.ppermute(
        obs,
        "tile",
        [(i, i + 1) for i in range(1, 31, 2)] + [(i + 1, i) for i in range(1, 31, 2)],
    )
    own5, own7, own2 = send(own4, 1), send(own4, 3), send(own3, 1)
    far4, far1, far3 = send(far0, 4), send(far0, 1), send(far0, 3)
    own6 = send(own5, 3)
    far5, far7 = send(far4, 1), send(far4, 3)
    far1, far3, own4 = hold((far1, far3, own4))
    table = own_table(where, (obs, own4, own1, own3, own5, own7, own2, own6))
    table, four, one = hold((table, pieces[4], pieces[1]))
    sibling = swap_cores(table)
    got[4] = send(four, 4)
    far2, far6 = send(far3, 1), send(far5, 3)
    far5, far7, *rest = hold((far5, far7, one, pieces[3]))
    got[1], got[3] = send(rest[0], 1), send(rest[1], 3)
    far2, sibling, got[4], *rest = hold((far2, sibling, got[4], pieces[2], *pieces[5:]))
    for s, x in zip((2, 5, 6, 7), rest):
        got[s] = send(x, s)
    far = (far0, far4, far1, far3, far5, far7, far2, far6)
    root, offset = find_mixing(where, nearby.T, damping.T, table, sibling, far)
    return apply_mixing(where, root, offset, got)


def solution(mesh):
    in_specs = (
        P("mem", None, "tile"),
        P(),
        P(("tile", "mem"), None),
        P(("tile", "mem"), None),
        P(("tile", "mem"), None),
        P(("tile", "mem"), None),
    )
    out_specs = P(None, None, ("tile", "mem"))
    return jax.shard_map(local, mesh=mesh, in_specs=in_specs, out_specs=out_specs, check_vma=False)
```

```python
import jax
import jax.numpy as jnp
from jax import lax
from jax.experimental import pallas as pl
from jax.experimental.pallas import tpu as pltpu
from jax.sharding import PartitionSpec as P

F32 = jnp.float32
BF16 = jnp.bfloat16
MEM = 8
LANES = 128
WIDE = 4
LIMIT = 62 << 20
VMEM = pl.BlockSpec(memory_space=pltpu.VMEM)
SMEM = pl.BlockSpec(memory_space=pltpu.SMEM)
ANYWHERE = pl.BlockSpec(memory_space=pl.ANY)
HBM = pl.BlockSpec(memory_space=pltpu.HBM)


def split(x):
    hi = x.astype(BF16)
    lo = (x - hi.astype(F32)).astype(BF16)
    return hi, lo


def dot(a, b):
    return jnp.dot(a, b, preferred_element_type=F32)


def dot_nt(a, b):
    return lax.dot_general(a, b, (((1,), (1,)), ((), ())), preferred_element_type=F32)


def mul3(a, b):
    (ah, al), (bh, bl) = a, b
    return dot(ah, bh) + (dot(ah, bl) + dot(al, bh))


def exchange_lanes(parts, first, second):
    out = list(parts)
    for bit, shift, odd in ((1, 32, first), (2, 64, second)):
        for low in range(4):
            if low & bit:
                continue
            a, b = out[low], out[low | bit]
            out[low] = jnp.where(odd, pltpu.roll(b, shift, 1), a)
            out[low | bit] = jnp.where(odd, b, pltpu.roll(a, LANES - shift, 1))
    return out


def lane_bits(rows):
    lane = lax.broadcasted_iota(jnp.int32, (rows, LANES), 1)
    return (lane // 32) % 2 == 1, lane // 64 == 1


def obs_kernel(where_ref, prior_ref, map_ref, reading_ref, noise_ref, *refs):
    pieces, obs_ref = refs[:MEM], refs[MEM]
    part, staged, stack, map_in, reading_in, noise_in, in_sems, out_sems = refs[MEM + 1 :]
    members = prior_ref.shape[0]
    me = where_ref[0]
    reads = []
    for s in range(MEM):
        cells = pl.ds(pl.multiple_of((me ^ s) * 512, 512), 512)
        reads.append(pltpu.make_async_copy(prior_ref.at[:, :, cells], part.at[s], in_sems.at[s]))
    for at, (source, target) in enumerate(
        ((map_ref, map_in), (reading_ref, reading_in), (noise_ref, noise_in))
    ):
        reads.append(pltpu.make_async_copy(source, target, in_sems.at[MEM + at]))
    writes = [
        pltpu.make_async_copy(staged.at[s], pieces[s], out_sems.at[s]) for s in range(MEM)
    ]
    for read in reads:
        read.start()
    first, second = lane_bits(members)
    for s in range(MEM):
        peer = me ^ s
        reads[s].wait()
        for c in range(4):
            lanes = slice(c * LANES, (c + 1) * LANES)
            layers = [part[s, :, l, lanes] for l in range(4)]
            groups = exchange_lanes(layers, first, second)
            for g in range(4):
                at = c * 4 + g
                staged[s, :, at * LANES : (at + 1) * LANES] = groups[g]
                row = pl.multiple_of((peer * 2 + at // 8) * members, members)
                stack[pl.ds(row, members), (at % 8) * LANES : (at % 8 + 1) * LANES] = groups[g]
        writes[s].start()
    for read in reads[MEM:]:
        read.wait()
    halves = [map_in[l, :, 32 * h : 32 * h + 32] for h in range(2) for l in range(4)]
    thin = jnp.concatenate(halves, axis=1)
    tall = jnp.concatenate([thin] * 4, axis=0)
    big = jnp.concatenate([tall] * 4, axis=1)
    row = lax.broadcasted_iota(jnp.int32, big.shape, 0)
    lane = lax.broadcasted_iota(jnp.int32, big.shape, 1)
    weights = jnp.where(lane // 256 == row // 32, big, 0.0)
    (xh, xl), (wh, wl) = split(stack[...]), split(weights)
    values = dot_nt(xh, wh) + (dot_nt(xh, wl) + dot_nt(xl, wh))
    for q in range(16):
        obs_ref[:, q * LANES : (q + 1) * LANES] = values[q * members : (q + 1) * members]
    obs_ref[:, 2048:2176] = jnp.zeros((members, LANES), F32)
    for at, ref in enumerate((reading_in, noise_in)):
        for half in range(2):
            line = [ref[half * 4 + j : half * 4 + j + 1, :] for j in range(4)]
            at_row = at * 2 + half
            obs_ref[at_row : at_row + 1, 2048:2176] = jnp.concatenate(line, axis=1)
    for write in writes:
        write.wait()


def local_obs(where, prior, measurement_map, readings, noise):
    members = prior.shape[0]
    return pl.pallas_call(
        obs_kernel,
        out_shape=[jax.ShapeDtypeStruct((members, 2048), F32)] * MEM
        + [jax.ShapeDtypeStruct((members, 2176), F32)],
        in_specs=[SMEM] + [HBM] * 4,
        out_specs=[HBM] * MEM + [VMEM],
        scratch_shapes=[
            pltpu.VMEM((MEM, members, 4, 512), F32),
            pltpu.VMEM((MEM, members, 2048), F32),
            pltpu.VMEM((512, 1024), F32),
            pltpu.VMEM(measurement_map.shape, F32),
            pltpu.VMEM(readings.shape, F32),
            pltpu.VMEM(noise.shape, F32),
            pltpu.SemaphoreType.DMA((MEM + 3,)),
            pltpu.SemaphoreType.DMA((MEM,)),
        ],
        compiler_params=pltpu.CompilerParams(vmem_limit_bytes=LIMIT),
        name="local_obs",
    )(where, prior, measurement_map, readings, noise)


def square(p):
    h, l = p
    m = dot(h, l)
    return dot(h, h) + (m + dot(l, h))


def each(function, *lists):
    return [function(*items) for items in zip(*lists)]


PLACES = (0, 4, 1, 3, 5, 7, 2, 6)


def placing(me, sources, raw, sems):
    return [
        pltpu.make_async_copy(
            source, raw.at[pl.ds(pl.multiple_of((me ^ x) * 32, 32), 32), :], sems.at[at]
        )
        for at, (x, source) in enumerate(zip(PLACES, sources))
    ]


def scale_tile(raw, table, first):
    extras = [raw[32 * m : 32 * m + 8, 2048:2176] for m in range(MEM)]
    reading = jnp.concatenate([e[i : i + 1] for e in extras for i in (0, 1)], axis=1)
    noise = jnp.concatenate([e[i : i + 1] for e in extras for i in (2, 3)], axis=1)
    scale = 1.0 / jnp.sqrt(noise)
    for c in range(16):
        lanes = slice(c * LANES, (c + 1) * LANES)
        value = raw[:, lanes]
        mean = jnp.sum(value, axis=0, keepdims=True) * (1.0 / 256.0)
        table[first + c, 0:256, :] = (value - mean) * scale[:, lanes]
        table[first + c, 256:264, :] = jnp.broadcast_to(
            (reading[:, lanes] - mean) * scale[:, lanes], (8, LANES)
        )


def table_kernel(where_ref, *refs):
    table_ref, raw, sems = refs[MEM:]
    copies = placing(where_ref[0], refs[:MEM], raw, sems)
    for copy in copies:
        copy.start()
    for copy in copies:
        copy.wait()
    scale_tile(raw, table_ref, 0)


def own_table(where, parts):
    return pl.pallas_call(
        table_kernel,
        out_shape=jax.ShapeDtypeStruct((16, 264, LANES), F32),
        in_specs=[SMEM] + [ANYWHERE] * MEM,
        out_specs=VMEM,
        scratch_shapes=[pltpu.VMEM((256, 2176), F32), pltpu.SemaphoreType.DMA((MEM,))],
        compiler_params=pltpu.CompilerParams(vmem_limit_bytes=12 << 20),
        cost_estimate=pl.CostEstimate(
            flops=4 * 256 * 2048, bytes_accessed=6 << 20, transcendentals=2048
        ),
        name="own_table",
    )(where, *parts)


def mixing_kernel(*refs):
    where_ref, near_ref, damp_ref, own_ref, sib_ref = refs[:5]
    far = refs[5 : 5 + MEM]
    root_ref, offset_ref, raw, table, sems = refs[5 + MEM :]

    @pl.when(pl.program_id(0) == 0)
    def gather():
        copies = placing(where_ref[0], far, raw, sems)
        for at, source in enumerate((own_ref, sib_ref)):
            copies.append(
                pltpu.make_async_copy(
                    source, table.at[pl.ds(at * 16, 16)], sems.at[MEM + at]
                )
            )
        for copy in copies:
            copy.start()
        for copy in copies[:MEM]:
            copy.wait()
        scale_tile(raw, table, 32)
        offset_ref[...] = jnp.zeros((256, LANES), F32)
        for copy in copies[MEM:]:
            copy.wait()

    rows = lax.broadcasted_iota(jnp.int32, (256, 256), 0)
    cols = lax.broadcasted_iota(jnp.int32, (256, 256), 1)
    diagonal = rows == cols
    block = lax.broadcasted_iota(jnp.int32, (1, LANES), 1) // 32
    lane = lax.broadcasted_iota(jnp.int32, (256, LANES), 1)

    def pick(g):
        halves = []
        for h in range(2):
            piece = jnp.zeros((264, LANES), F32)
            level = jnp.zeros((1, LANES), jnp.int32)
            for i in range(4):
                entry = near_ref[4 * h + i, g]
                tile = lax.shift_right_logical(entry, 6)
                other = jnp.where((tile ^ where_ref[1]) == 1, 16, 32)
                chunk = jnp.where(tile == where_ref[1], 0, other) + (
                    lax.shift_right_logical(entry, 2) & 15
                )
                shift = ((i - entry) & 3) * 32
                moved = pltpu.roll(table[chunk], shift, 1)
                piece = jnp.where(block == i, moved, piece)
                level = jnp.where(block == i, damp_ref[4 * h + i, g], level)
            halves.append(piece * jnp.sqrt(1.0 / (1.0 + level.astype(F32))))
        return jnp.concatenate(halves, axis=1)

    groups = [pl.program_id(0) * WIDE + u for u in range(WIDE)]
    picked = each(pick, groups)
    drives = each(
        lambda p: jnp.sum(p[0:256] * p[256:257], axis=1, keepdims=True), picked
    )
    parts = each(lambda p: split(p[0:256]), picked)
    grams = each(
        lambda p: dot_nt(p[0], p[0]) + (dot_nt(p[0], p[1]) + dot_nt(p[1], p[0])), parts
    )
    grams = each(lambda g: g + jnp.where(diagonal, 255.0, 0.0), grams)
    inverses = each(
        lambda g: 1.0
        / jnp.max(jnp.sum(jnp.abs(g), axis=0, keepdims=True), axis=1, keepdims=True),
        grams,
    )
    current = each(lambda g, v: g * v, grams, inverses)
    roots = []
    for step in range(3):
        parts = each(split, current)
        second = each(square, parts)
        if step < 2:
            products = each(mul3, parts, each(split, second))
        if step != 1:
            mixed = each(lambda s, c: split(s - 4.5 * c), second, current)
            roots.append(
                each(
                    lambda m, s, c: 0.0625 * square(m)
                    + (0.421875 * s - 2.4375 * c + jnp.where(diagonal, 2.25, 0.0)),
                    mixed,
                    second,
                    current,
                )
            )
        if step < 2:
            current = each(
                lambda c, s, p: 2.25 * c - 1.5 * s + 0.25 * p, current, second, products
            )
    root = each(mul3, each(split, roots[0]), each(split, roots[1]))
    inner = each(lambda r, d: jnp.sum(r * d, axis=0, keepdims=True), root, drives)
    offsets = each(
        lambda r, n, v: jnp.sum(r * n, axis=1, keepdims=True) * v, root, inner, inverses
    )
    held = offset_ref[...]
    for u, (g, r, v, o) in enumerate(zip(groups, root, inverses, offsets)):
        root_ref[u] = jnp.sqrt(255.0 * v) * r
        held = jnp.where(lane == g, o, held)
    offset_ref[...] = held


def apply_kernel(where_ref, root_ref, offset_ref, *refs):
    pieces = refs[:MEM]
    out_ref, field, sems = refs[MEM:]
    me = where_ref[0]

    @pl.when(pl.program_id(0) == 0)
    def gather():
        copies = [
            pltpu.make_async_copy(
                pieces[s], field.at[pl.ds(pl.multiple_of((me ^ s) * 32, 32), 32), :], sems.at[s]
            )
            for s in range(MEM)
        ]
        for copy in copies:
            copy.start()
        for copy in copies:
            copy.wait()

    odd, high = lane_bits(256)
    lane = lax.broadcasted_iota(jnp.int32, (256, LANES), 1)
    groups = [pl.program_id(0) * 4 + g for g in range(4)]
    value = [field[:, pl.ds(pl.multiple_of(g * LANES, LANES), LANES)] for g in groups]
    centre = each(lambda x: jnp.sum(x, axis=0, keepdims=True) * (1.0 / 256.0), value)
    anomaly = each(lambda x, a: x - a, value, centre)
    offset = [
        jnp.sum(jnp.where(lane == g, offset_ref[...], 0.0), axis=1, keepdims=True) for g in groups
    ]
    base = each(
        lambda a, x, o: a + jnp.sum(x * o, axis=0, keepdims=True), centre, anomaly, offset
    )
    spread = each(mul3, [split(root_ref[u]) for u in range(4)], each(split, anomaly))
    layers = exchange_lanes(each(lambda b, x: b + x, base, spread), odd, high)
    for l in range(4):
        out_ref[:, l, :] = layers[l]


def find_mixing(where, nearby, damping, own, sib, far):
    return pl.pallas_call(
        mixing_kernel,
        out_shape=[
            jax.ShapeDtypeStruct((16, 256, 256), F32),
            jax.ShapeDtypeStruct((256, LANES), F32),
        ],
        grid=(16 // WIDE,),
        in_specs=[SMEM] * 3 + [ANYWHERE] * (2 + MEM),
        out_specs=[
            pl.BlockSpec((WIDE, 256, 256), lambda i: (i, 0, 0)),
            pl.BlockSpec((256, LANES), lambda i: (0, 0)),
        ],
        scratch_shapes=[
            pltpu.VMEM((256, 2176), F32),
            pltpu.VMEM((48, 264, LANES), F32),
            pltpu.SemaphoreType.DMA((MEM + 2,)),
        ],
        compiler_params=pltpu.CompilerParams(vmem_limit_bytes=30 << 20),
        cost_estimate=pl.CostEstimate(
            flops=16 * 30 * 2 * 256**3, bytes_accessed=12 << 20, transcendentals=0
        ),
        name="mixing",
    )(where, nearby, damping, own, sib, *far)


def apply_mixing(where, root, offset, pieces):
    return pl.pallas_call(
        apply_kernel,
        out_shape=jax.ShapeDtypeStruct((256, 4, 512), F32),
        grid=(4,),
        in_specs=[SMEM, pl.BlockSpec((4, 256, 256), lambda i: (i, 0, 0)), VMEM] + [ANYWHERE] * MEM,
        out_specs=pl.BlockSpec((256, 4, LANES), lambda i: (0, 0, i)),
        scratch_shapes=[pltpu.VMEM((256, 2048), F32), pltpu.SemaphoreType.DMA((MEM,))],
        compiler_params=pltpu.CompilerParams(vmem_limit_bytes=30 << 20),
        name="apply",
    )(where, root, offset, *pieces)


def send(x, flip):
    return lax.ppermute(x, "mem", [(i, i ^ flip) for i in range(MEM)])


def swap_cores(x):
    return lax.ppermute(x, "tile", [(i, i ^ 1) for i in range(32)])


def local(prior, measurement_matrix, readings, noise, nearby, damping):
    me = lax.axis_index("mem").astype(jnp.int32)
    tile = lax.axis_index("tile").astype(jnp.int32)
    where = jnp.stack([me, tile])
    measurement_map = jnp.swapaxes(measurement_matrix, 1, 2)
    *pieces, obs = local_obs(where, prior, measurement_map, readings, noise)
    hold = lax.optimization_barrier
    got = [pieces[0]] + [None] * 7
    own4, own1, own3 = send(obs, 4), send(obs, 1), send(obs, 3)
    far0 = lax.ppermute(
        obs,
        "tile",
        [(i, i + 1) for i in range(1, 31, 2)] + [(i + 1, i) for i in range(1, 31, 2)],
    )
    own5, own7, own2 = send(own4, 1), send(own4, 3), send(own3, 1)
    far4, far1, far3 = send(far0, 4), send(far0, 1), send(far0, 3)
    own6 = send(own5, 3)
    far1, far3, far4, own4 = hold((far1, far3, far4, own4))
    far5, far7 = send(far4, 1), send(far4, 3)
    table = own_table(where, (obs, own4, own1, own3, own5, own7, own2, own6))
    table, four, one = hold((table, pieces[4], pieces[1]))
    sibling = swap_cores(table)
    got[4] = send(four, 4)
    far2, far6 = send(far3, 1), send(far5, 3)
    far5, far7, *rest = hold((far5, far7, one, pieces[3]))
    got[1], got[3] = send(rest[0], 1), send(rest[1], 3)
    far2, sibling, got[4], *rest = hold((far2, sibling, got[4], pieces[2], *pieces[5:]))
    for s, x in zip((2, 5, 6, 7), rest):
        got[s] = send(x, s)
    far = (far0, far4, far1, far3, far5, far7, far2, far6)
    root, offset = find_mixing(where, nearby.T, damping.T, table, sibling, far)
    return apply_mixing(where, root, offset, got)


def solution(mesh):
    in_specs = (
        P("mem", None, "tile"),
        P(),
        P(("tile", "mem"), None),
        P(("tile", "mem"), None),
        P(("tile", "mem"), None),
        P(("tile", "mem"), None),
    )
    out_specs = P(None, None, ("tile", "mem"))
    return jax.shard_map(local, mesh=mesh, in_specs=in_specs, out_specs=out_specs, check_vma=False)
```

```python
import jax
import jax.numpy as jnp
from jax import lax
from jax.experimental import pallas as pl
from jax.experimental.pallas import tpu as pltpu
from jax.sharding import PartitionSpec as P

F32 = jnp.float32
BF16 = jnp.bfloat16
MEM = 8
LANES = 128
WIDE = 8
LIMIT = 62 << 20
VMEM = pl.BlockSpec(memory_space=pltpu.VMEM)
SMEM = pl.BlockSpec(memory_space=pltpu.SMEM)
ANYWHERE = pl.BlockSpec(memory_space=pl.ANY)
HBM = pl.BlockSpec(memory_space=pltpu.HBM)


def split(x):
    hi = x.astype(BF16)
    lo = (x - hi.astype(F32)).astype(BF16)
    return hi, lo


def dot(a, b):
    return jnp.dot(a, b, preferred_element_type=F32)


def dot_nt(a, b):
    return lax.dot_general(a, b, (((1,), (1,)), ((), ())), preferred_element_type=F32)


def mul3(a, b):
    (ah, al), (bh, bl) = a, b
    return dot(ah, bh) + (dot(ah, bl) + dot(al, bh))


def exchange_lanes(parts, first, second):
    out = list(parts)
    for bit, shift, odd in ((1, 32, first), (2, 64, second)):
        for low in range(4):
            if low & bit:
                continue
            a, b = out[low], out[low | bit]
            out[low] = jnp.where(odd, pltpu.roll(b, shift, 1), a)
            out[low | bit] = jnp.where(odd, b, pltpu.roll(a, LANES - shift, 1))
    return out


def lane_bits(rows):
    lane = lax.broadcasted_iota(jnp.int32, (rows, LANES), 1)
    return (lane // 32) % 2 == 1, lane // 64 == 1


def obs_kernel(where_ref, prior_ref, map_ref, reading_ref, noise_ref, *refs):
    pieces, obs_ref = refs[:MEM], refs[MEM]
    part, staged, stack, map_in, reading_in, noise_in, in_sems, out_sems = refs[MEM + 1 :]
    members = prior_ref.shape[0]
    me = where_ref[0]
    reads = []
    for s in range(MEM):
        cells = pl.ds(pl.multiple_of((me ^ s) * 512, 512), 512)
        reads.append(pltpu.make_async_copy(prior_ref.at[:, :, cells], part.at[s], in_sems.at[s]))
    for at, (source, target) in enumerate(
        ((map_ref, map_in), (reading_ref, reading_in), (noise_ref, noise_in))
    ):
        reads.append(pltpu.make_async_copy(source, target, in_sems.at[MEM + at]))
    writes = [
        pltpu.make_async_copy(staged.at[s], pieces[s], out_sems.at[s]) for s in range(MEM)
    ]
    for read in reads:
        read.start()
    first, second = lane_bits(members)
    for s in range(MEM):
        peer = me ^ s
        reads[s].wait()
        for c in range(4):
            lanes = slice(c * LANES, (c + 1) * LANES)
            layers = [part[s, :, l, lanes] for l in range(4)]
            groups = exchange_lanes(layers, first, second)
            for g in range(4):
                at = c * 4 + g
                staged[s, :, at * LANES : (at + 1) * LANES] = groups[g]
                row = pl.multiple_of((peer * 2 + at // 8) * members, members)
                stack[pl.ds(row, members), (at % 8) * LANES : (at % 8 + 1) * LANES] = groups[g]
        writes[s].start()
    for read in reads[MEM:]:
        read.wait()
    halves = [map_in[l, :, 32 * h : 32 * h + 32] for h in range(2) for l in range(4)]
    thin = jnp.concatenate(halves, axis=1)
    tall = jnp.concatenate([thin] * 4, axis=0)
    big = jnp.concatenate([tall] * 4, axis=1)
    row = lax.broadcasted_iota(jnp.int32, big.shape, 0)
    lane = lax.broadcasted_iota(jnp.int32, big.shape, 1)
    weights = jnp.where(lane // 256 == row // 32, big, 0.0)
    (xh, xl), (wh, wl) = split(stack[...]), split(weights)
    values = dot_nt(xh, wh) + (dot_nt(xh, wl) + dot_nt(xl, wh))
    for q in range(16):
        obs_ref[:, q * LANES : (q + 1) * LANES] = values[q * members : (q + 1) * members]
    obs_ref[:, 2048:2176] = jnp.zeros((members, LANES), F32)
    for at, ref in enumerate((reading_in, noise_in)):
        for half in range(2):
            line = [ref[half * 4 + j : half * 4 + j + 1, :] for j in range(4)]
            at_row = at * 2 + half
            obs_ref[at_row : at_row + 1, 2048:2176] = jnp.concatenate(line, axis=1)
    for write in writes:
        write.wait()


def local_obs(where, prior, measurement_map, readings, noise):
    members = prior.shape[0]
    return pl.pallas_call(
        obs_kernel,
        out_shape=[jax.ShapeDtypeStruct((members, 2048), F32)] * MEM
        + [jax.ShapeDtypeStruct((members, 2176), F32)],
        in_specs=[SMEM] + [HBM] * 4,
        out_specs=[HBM] * MEM + [VMEM],
        scratch_shapes=[
            pltpu.VMEM((MEM, members, 4, 512), F32),
            pltpu.VMEM((MEM, members, 2048), F32),
            pltpu.VMEM((512, 1024), F32),
            pltpu.VMEM(measurement_map.shape, F32),
            pltpu.VMEM(readings.shape, F32),
            pltpu.VMEM(noise.shape, F32),
            pltpu.SemaphoreType.DMA((MEM + 3,)),
            pltpu.SemaphoreType.DMA((MEM,)),
        ],
        compiler_params=pltpu.CompilerParams(vmem_limit_bytes=LIMIT),
        name="local_obs",
    )(where, prior, measurement_map, readings, noise)


def square(p):
    h, l = p
    m = dot(h, l)
    return dot(h, h) + (m + dot(l, h))


def each(function, *lists):
    return [function(*items) for items in zip(*lists)]


PLACES = (0, 4, 1, 3, 5, 7, 2, 6)


def placing(me, sources, raw, sems):
    return [
        pltpu.make_async_copy(
            source, raw.at[pl.ds(pl.multiple_of((me ^ x) * 32, 32), 32), :], sems.at[at]
        )
        for at, (x, source) in enumerate(zip(PLACES, sources))
    ]


def scale_tile(raw, table, first):
    extras = [raw[32 * m : 32 * m + 8, 2048:2176] for m in range(MEM)]
    reading = jnp.concatenate([e[i : i + 1] for e in extras for i in (0, 1)], axis=1)
    noise = jnp.concatenate([e[i : i + 1] for e in extras for i in (2, 3)], axis=1)
    scale = 1.0 / jnp.sqrt(noise)
    for c in range(16):
        lanes = slice(c * LANES, (c + 1) * LANES)
        value = raw[:, lanes]
        mean = jnp.sum(value, axis=0, keepdims=True) * (1.0 / 256.0)
        table[first + c, 0:256, :] = (value - mean) * scale[:, lanes]
        table[first + c, 256:264, :] = jnp.broadcast_to(
            (reading[:, lanes] - mean) * scale[:, lanes], (8, LANES)
        )


def table_kernel(where_ref, *refs):
    table_ref, raw, sems = refs[MEM:]
    copies = placing(where_ref[0], refs[:MEM], raw, sems)
    for copy in copies:
        copy.start()
    for copy in copies:
        copy.wait()
    scale_tile(raw, table_ref, 0)


def own_table(where, parts):
    return pl.pallas_call(
        table_kernel,
        out_shape=jax.ShapeDtypeStruct((16, 264, LANES), F32),
        in_specs=[SMEM] + [ANYWHERE] * MEM,
        out_specs=VMEM,
        scratch_shapes=[pltpu.VMEM((256, 2176), F32), pltpu.SemaphoreType.DMA((MEM,))],
        compiler_params=pltpu.CompilerParams(vmem_limit_bytes=12 << 20),
        cost_estimate=pl.CostEstimate(
            flops=4 * 256 * 2048, bytes_accessed=6 << 20, transcendentals=2048
        ),
        name="own_table",
    )(where, *parts)


def mixing_kernel(*refs):
    where_ref, near_ref, damp_ref, own_ref, sib_ref = refs[:5]
    far = refs[5 : 5 + MEM]
    root_ref, offset_ref, raw, table, sems = refs[5 + MEM :]

    @pl.when(pl.program_id(0) == 0)
    def gather():
        copies = placing(where_ref[0], far, raw, sems)
        for at, source in enumerate((own_ref, sib_ref)):
            copies.append(
                pltpu.make_async_copy(
                    source, table.at[pl.ds(at * 16, 16)], sems.at[MEM + at]
                )
            )
        for copy in copies:
            copy.start()
        for copy in copies[:MEM]:
            copy.wait()
        scale_tile(raw, table, 32)
        offset_ref[...] = jnp.zeros((256, LANES), F32)
        for copy in copies[MEM:]:
            copy.wait()

    rows = lax.broadcasted_iota(jnp.int32, (256, 256), 0)
    cols = lax.broadcasted_iota(jnp.int32, (256, 256), 1)
    diagonal = rows == cols
    block = lax.broadcasted_iota(jnp.int32, (1, LANES), 1) // 32
    lane = lax.broadcasted_iota(jnp.int32, (256, LANES), 1)

    def pick(g):
        halves = []
        for h in range(2):
            piece = jnp.zeros((264, LANES), F32)
            level = jnp.zeros((1, LANES), jnp.int32)
            for i in range(4):
                entry = near_ref[4 * h + i, g]
                tile = lax.shift_right_logical(entry, 6)
                other = jnp.where((tile ^ where_ref[1]) == 1, 16, 32)
                chunk = jnp.where(tile == where_ref[1], 0, other) + (
                    lax.shift_right_logical(entry, 2) & 15
                )
                shift = ((i - entry) & 3) * 32
                moved = pltpu.roll(table[chunk], shift, 1)
                piece = jnp.where(block == i, moved, piece)
                level = jnp.where(block == i, damp_ref[4 * h + i, g], level)
            halves.append(piece * jnp.sqrt(1.0 / (1.0 + level.astype(F32))))
        return jnp.concatenate(halves, axis=1)

    groups = [pl.program_id(0) * WIDE + u for u in range(WIDE)]
    picked = each(pick, groups)
    drives = each(
        lambda p: jnp.sum(p[0:256] * p[256:257], axis=1, keepdims=True), picked
    )
    parts = each(lambda p: split(p[0:256]), picked)
    grams = each(
        lambda p: dot_nt(p[0], p[0]) + (dot_nt(p[0], p[1]) + dot_nt(p[1], p[0])), parts
    )
    grams = each(lambda g: g + jnp.where(diagonal, 255.0, 0.0), grams)
    inverses = each(
        lambda g: 1.0
        / jnp.max(jnp.sum(jnp.abs(g), axis=0, keepdims=True), axis=1, keepdims=True),
        grams,
    )
    current = each(lambda g, v: g * v, grams, inverses)
    roots = []
    for step in range(3):
        parts = each(split, current)
        second = each(square, parts)
        if step < 2:
            products = each(mul3, parts, each(split, second))
        if step != 1:
            mixed = each(lambda s, c: split(s - 4.5 * c), second, current)
            roots.append(
                each(
                    lambda m, s, c: 0.0625 * square(m)
                    + (0.421875 * s - 2.4375 * c + jnp.where(diagonal, 2.25, 0.0)),
                    mixed,
                    second,
                    current,
                )
            )
        if step < 2:
            current = each(
                lambda c, s, p: 2.25 * c - 1.5 * s + 0.25 * p, current, second, products
            )
    root = each(mul3, each(split, roots[0]), each(split, roots[1]))
    inner = each(lambda r, d: jnp.sum(r * d, axis=0, keepdims=True), root, drives)
    offsets = each(
        lambda r, n, v: jnp.sum(r * n, axis=1, keepdims=True) * v, root, inner, inverses
    )
    held = offset_ref[...]
    for u, (g, r, v, o) in enumerate(zip(groups, root, inverses, offsets)):
        root_ref[u] = jnp.sqrt(255.0 * v) * r
        held = jnp.where(lane == g, o, held)
    offset_ref[...] = held


def apply_kernel(where_ref, root_ref, offset_ref, *refs):
    pieces = refs[:MEM]
    out_ref, field, sems = refs[MEM:]
    me = where_ref[0]

    @pl.when(pl.program_id(0) == 0)
    def gather():
        copies = [
            pltpu.make_async_copy(
                pieces[s], field.at[pl.ds(pl.multiple_of((me ^ s) * 32, 32), 32), :], sems.at[s]
            )
            for s in range(MEM)
        ]
        for copy in copies:
            copy.start()
        for copy in copies:
            copy.wait()

    odd, high = lane_bits(256)
    lane = lax.broadcasted_iota(jnp.int32, (256, LANES), 1)
    groups = [pl.program_id(0) * 4 + g for g in range(4)]
    value = [field[:, pl.ds(pl.multiple_of(g * LANES, LANES), LANES)] for g in groups]
    centre = each(lambda x: jnp.sum(x, axis=0, keepdims=True) * (1.0 / 256.0), value)
    anomaly = each(lambda x, a: x - a, value, centre)
    offset = [
        jnp.sum(jnp.where(lane == g, offset_ref[...], 0.0), axis=1, keepdims=True) for g in groups
    ]
    base = each(
        lambda a, x, o: a + jnp.sum(x * o, axis=0, keepdims=True), centre, anomaly, offset
    )
    spread = each(mul3, [split(root_ref[u]) for u in range(4)], each(split, anomaly))
    layers = exchange_lanes(each(lambda b, x: b + x, base, spread), odd, high)
    for l in range(4):
        out_ref[:, l, :] = layers[l]


def find_mixing(where, nearby, damping, own, sib, far):
    return pl.pallas_call(
        mixing_kernel,
        out_shape=[
            jax.ShapeDtypeStruct((16, 256, 256), F32),
            jax.ShapeDtypeStruct((256, LANES), F32),
        ],
        grid=(16 // WIDE,),
        in_specs=[SMEM] * 3 + [ANYWHERE] * (2 + MEM),
        out_specs=[
            pl.BlockSpec((WIDE, 256, 256), lambda i: (i, 0, 0)),
            pl.BlockSpec((256, LANES), lambda i: (0, 0)),
        ],
        scratch_shapes=[
            pltpu.VMEM((256, 2176), F32),
            pltpu.VMEM((48, 264, LANES), F32),
            pltpu.SemaphoreType.DMA((MEM + 2,)),
        ],
        compiler_params=pltpu.CompilerParams(vmem_limit_bytes=42 << 20),
        cost_estimate=pl.CostEstimate(
            flops=16 * 30 * 2 * 256**3, bytes_accessed=12 << 20, transcendentals=0
        ),
        name="mixing",
    )(where, nearby, damping, own, sib, *far)


def apply_mixing(where, root, offset, pieces):
    return pl.pallas_call(
        apply_kernel,
        out_shape=jax.ShapeDtypeStruct((256, 4, 512), F32),
        grid=(4,),
        in_specs=[SMEM, pl.BlockSpec((4, 256, 256), lambda i: (i, 0, 0)), VMEM] + [ANYWHERE] * MEM,
        out_specs=pl.BlockSpec((256, 4, LANES), lambda i: (0, 0, i)),
        scratch_shapes=[pltpu.VMEM((256, 2048), F32), pltpu.SemaphoreType.DMA((MEM,))],
        compiler_params=pltpu.CompilerParams(vmem_limit_bytes=30 << 20),
        name="apply",
    )(where, root, offset, *pieces)


def send(x, flip):
    return lax.ppermute(x, "mem", [(i, i ^ flip) for i in range(MEM)])


def swap_cores(x):
    return lax.ppermute(x, "tile", [(i, i ^ 1) for i in range(32)])


def local(prior, measurement_matrix, readings, noise, nearby, damping):
    me = lax.axis_index("mem").astype(jnp.int32)
    tile = lax.axis_index("tile").astype(jnp.int32)
    where = jnp.stack([me, tile])
    measurement_map = jnp.swapaxes(measurement_matrix, 1, 2)
    *pieces, obs = local_obs(where, prior, measurement_map, readings, noise)
    hold = lax.optimization_barrier
    got = [pieces[0]] + [None] * 7
    own4, own1, own3 = send(obs, 4), send(obs, 1), send(obs, 3)
    far0 = lax.ppermute(
        obs,
        "tile",
        [(i, i + 1) for i in range(1, 31, 2)] + [(i + 1, i) for i in range(1, 31, 2)],
    )
    own5, own7, own2 = send(own4, 1), send(own4, 3), send(own3, 1)
    far4, far1, far3 = send(far0, 4), send(far0, 1), send(far0, 3)
    own6 = send(own5, 3)
    far1, far3, far4, own4 = hold((far1, far3, far4, own4))
    far5, far7 = send(far4, 1), send(far4, 3)
    table = own_table(where, (obs, own4, own1, own3, own5, own7, own2, own6))
    table, four = hold((table, pieces[4]))
    got[4] = send(four, 4)
    far2 = send(far3, 1)
    far5, far7, table, one, three = hold((far5, far7, table, pieces[1], pieces[3]))
    far6, sibling = send(far5, 3), swap_cores(table)
    got[1], got[3] = send(one, 1), send(three, 3)
    far2, sibling, got[4], *rest = hold((far2, sibling, got[4], pieces[2], *pieces[5:]))
    for s, x in zip((2, 5, 6, 7), rest):
        got[s] = send(x, s)
    far = (far0, far4, far1, far3, far5, far7, far2, far6)
    root, offset = find_mixing(where, nearby.T, damping.T, table, sibling, far)
    return apply_mixing(where, root, offset, got)


def solution(mesh):
    in_specs = (
        P("mem", None, "tile"),
        P(),
        P(("tile", "mem"), None),
        P(("tile", "mem"), None),
        P(("tile", "mem"), None),
        P(("tile", "mem"), None),
    )
    out_specs = P(None, None, ("tile", "mem"))
    return jax.shard_map(local, mesh=mesh, in_specs=in_specs, out_specs=out_specs, check_vma=False)
```

```python
import jax
import jax.numpy as jnp
from jax import lax
from jax.experimental import pallas as pl
from jax.experimental.pallas import tpu as pltpu
from jax.sharding import PartitionSpec as P

F32 = jnp.float32
BF16 = jnp.bfloat16
MEM = 8
LANES = 128
WIDE = 8
LIMIT = 62 << 20
VMEM = pl.BlockSpec(memory_space=pltpu.VMEM)
SMEM = pl.BlockSpec(memory_space=pltpu.SMEM)
ANYWHERE = pl.BlockSpec(memory_space=pl.ANY)
HBM = pl.BlockSpec(memory_space=pltpu.HBM)


def split(x):
    hi = x.astype(BF16)
    lo = (x - hi.astype(F32)).astype(BF16)
    return hi, lo


def dot(a, b):
    return jnp.dot(a, b, preferred_element_type=F32)


def dot_nt(a, b):
    return lax.dot_general(a, b, (((1,), (1,)), ((), ())), preferred_element_type=F32)


def mul3(a, b):
    (ah, al), (bh, bl) = a, b
    return dot(ah, bh) + (dot(ah, bl) + dot(al, bh))


def exchange_lanes(parts, first, second):
    out = list(parts)
    for bit, shift, odd in ((1, 32, first), (2, 64, second)):
        for low in range(4):
            if low & bit:
                continue
            a, b = out[low], out[low | bit]
            out[low] = jnp.where(odd, pltpu.roll(b, shift, 1), a)
            out[low | bit] = jnp.where(odd, b, pltpu.roll(a, LANES - shift, 1))
    return out


def lane_bits(rows):
    lane = lax.broadcasted_iota(jnp.int32, (rows, LANES), 1)
    return (lane // 32) % 2 == 1, lane // 64 == 1


def obs_kernel(where_ref, prior_ref, map_ref, reading_ref, noise_ref, *refs):
    pieces, obs_ref = refs[:MEM], refs[MEM]
    part, staged, stack, map_in, reading_in, noise_in, in_sems, out_sems = refs[MEM + 1 :]
    members = prior_ref.shape[0]
    me = where_ref[0]
    reads = []
    for s in range(MEM):
        cells = pl.ds(pl.multiple_of((me ^ s) * 512, 512), 512)
        reads.append(pltpu.make_async_copy(prior_ref.at[:, :, cells], part.at[s], in_sems.at[s]))
    for at, (source, target) in enumerate(
        ((map_ref, map_in), (reading_ref, reading_in), (noise_ref, noise_in))
    ):
        reads.append(pltpu.make_async_copy(source, target, in_sems.at[MEM + at]))
    writes = [
        pltpu.make_async_copy(staged.at[s], pieces[s], out_sems.at[s]) for s in range(MEM)
    ]
    for read in reads:
        read.start()
    first, second = lane_bits(members)
    for s in range(MEM):
        peer = me ^ s
        reads[s].wait()
        for c in range(4):
            lanes = slice(c * LANES, (c + 1) * LANES)
            layers = [part[s, :, l, lanes] for l in range(4)]
            groups = exchange_lanes(layers, first, second)
            for g in range(4):
                at = c * 4 + g
                staged[s, :, at * LANES : (at + 1) * LANES] = groups[g]
                row = pl.multiple_of((peer * 2 + at // 8) * members, members)
                stack[pl.ds(row, members), (at % 8) * LANES : (at % 8 + 1) * LANES] = groups[g]
        writes[s].start()
    for read in reads[MEM:]:
        read.wait()
    halves = [map_in[l, :, 32 * h : 32 * h + 32] for h in range(2) for l in range(4)]
    thin = jnp.concatenate(halves, axis=1)
    tall = jnp.concatenate([thin] * 4, axis=0)
    big = jnp.concatenate([tall] * 4, axis=1)
    row = lax.broadcasted_iota(jnp.int32, big.shape, 0)
    lane = lax.broadcasted_iota(jnp.int32, big.shape, 1)
    weights = jnp.where(lane // 256 == row // 32, big, 0.0)
    (xh, xl), (wh, wl) = split(stack[...]), split(weights)
    values = dot_nt(xh, wh) + (dot_nt(xh, wl) + dot_nt(xl, wh))
    for q in range(16):
        obs_ref[:, q * LANES : (q + 1) * LANES] = values[q * members : (q + 1) * members]
    obs_ref[:, 2048:2176] = jnp.zeros((members, LANES), F32)
    for at, ref in enumerate((reading_in, noise_in)):
        for half in range(2):
            line = [ref[half * 4 + j : half * 4 + j + 1, :] for j in range(4)]
            at_row = at * 2 + half
            obs_ref[at_row : at_row + 1, 2048:2176] = jnp.concatenate(line, axis=1)
    for write in writes:
        write.wait()


def local_obs(where, prior, measurement_map, readings, noise):
    members = prior.shape[0]
    return pl.pallas_call(
        obs_kernel,
        out_shape=[jax.ShapeDtypeStruct((members, 2048), F32)] * MEM
        + [jax.ShapeDtypeStruct((members, 2176), F32)],
        in_specs=[SMEM] + [HBM] * 4,
        out_specs=[HBM] * MEM + [VMEM],
        scratch_shapes=[
            pltpu.VMEM((MEM, members, 4, 512), F32),
            pltpu.VMEM((MEM, members, 2048), F32),
            pltpu.VMEM((512, 1024), F32),
            pltpu.VMEM(measurement_map.shape, F32),
            pltpu.VMEM(readings.shape, F32),
            pltpu.VMEM(noise.shape, F32),
            pltpu.SemaphoreType.DMA((MEM + 3,)),
            pltpu.SemaphoreType.DMA((MEM,)),
        ],
        compiler_params=pltpu.CompilerParams(vmem_limit_bytes=LIMIT),
        name="local_obs",
    )(where, prior, measurement_map, readings, noise)


def square(p):
    h, l = p
    m = dot(h, l)
    return dot(h, h) + (m + dot(l, h))


def each(function, *lists):
    return [function(*items) for items in zip(*lists)]


PLACES = (0, 4, 1, 3, 5, 7, 2, 6)


def placing(me, sources, raw, sems):
    return [
        pltpu.make_async_copy(
            source, raw.at[pl.ds(pl.multiple_of((me ^ x) * 32, 32), 32), :], sems.at[at]
        )
        for at, (x, source) in enumerate(zip(PLACES, sources))
    ]


def scale_tile(raw, table, first):
    extras = [raw[32 * m : 32 * m + 8, 2048:2176] for m in range(MEM)]
    reading = jnp.concatenate([e[i : i + 1] for e in extras for i in (0, 1)], axis=1)
    noise = jnp.concatenate([e[i : i + 1] for e in extras for i in (2, 3)], axis=1)
    scale = 1.0 / jnp.sqrt(noise)
    for c in range(16):
        lanes = slice(c * LANES, (c + 1) * LANES)
        value = raw[:, lanes]
        mean = jnp.sum(value, axis=0, keepdims=True) * (1.0 / 256.0)
        table[first + c, 0:256, :] = (value - mean) * scale[:, lanes]
        table[first + c, 256:264, :] = jnp.broadcast_to(
            (reading[:, lanes] - mean) * scale[:, lanes], (8, LANES)
        )


def table_kernel(where_ref, *refs):
    table_ref, raw, sems = refs[MEM:]
    copies = placing(where_ref[0], refs[:MEM], raw, sems)
    for copy in copies:
        copy.start()
    for copy in copies:
        copy.wait()
    scale_tile(raw, table_ref, 0)


def own_table(where, parts):
    return pl.pallas_call(
        table_kernel,
        out_shape=jax.ShapeDtypeStruct((16, 264, LANES), F32),
        in_specs=[SMEM] + [ANYWHERE] * MEM,
        out_specs=VMEM,
        scratch_shapes=[pltpu.VMEM((256, 2176), F32), pltpu.SemaphoreType.DMA((MEM,))],
        compiler_params=pltpu.CompilerParams(vmem_limit_bytes=12 << 20),
        cost_estimate=pl.CostEstimate(
            flops=4 * 256 * 2048, bytes_accessed=6 << 20, transcendentals=2048
        ),
        name="own_table",
    )(where, *parts)


def mixing_kernel(*refs):
    where_ref, near_ref, damp_ref, own_ref, sib_ref = refs[:5]
    far = refs[5 : 5 + MEM]
    root_ref, offset_ref, raw, table, sems = refs[5 + MEM :]

    @pl.when(pl.program_id(0) == 0)
    def gather():
        copies = placing(where_ref[0], far, raw, sems)
        for at, source in enumerate((own_ref, sib_ref)):
            copies.append(
                pltpu.make_async_copy(
                    source, table.at[pl.ds(at * 16, 16)], sems.at[MEM + at]
                )
            )
        for copy in copies:
            copy.start()
        for copy in copies[:MEM]:
            copy.wait()
        scale_tile(raw, table, 32)
        offset_ref[...] = jnp.zeros((256, LANES), F32)
        for copy in copies[MEM:]:
            copy.wait()

    rows = lax.broadcasted_iota(jnp.int32, (256, 256), 0)
    cols = lax.broadcasted_iota(jnp.int32, (256, 256), 1)
    diagonal = rows == cols
    block = lax.broadcasted_iota(jnp.int32, (1, LANES), 1) // 32
    lane = lax.broadcasted_iota(jnp.int32, (256, LANES), 1)

    def pick(g):
        halves = []
        for h in range(2):
            piece = jnp.zeros((264, LANES), F32)
            level = jnp.zeros((1, LANES), jnp.int32)
            for i in range(4):
                entry = near_ref[4 * h + i, g]
                tile = lax.shift_right_logical(entry, 6)
                other = jnp.where((tile ^ where_ref[1]) == 1, 16, 32)
                chunk = jnp.where(tile == where_ref[1], 0, other) + (
                    lax.shift_right_logical(entry, 2) & 15
                )
                shift = ((i - entry) & 3) * 32
                moved = pltpu.roll(table[chunk], shift, 1)
                piece = jnp.where(block == i, moved, piece)
                level = jnp.where(block == i, damp_ref[4 * h + i, g], level)
            halves.append(piece * jnp.sqrt(1.0 / (1.0 + level.astype(F32))))
        return jnp.concatenate(halves, axis=1)

    groups = [pl.program_id(0) * WIDE + u for u in range(WIDE)]
    picked = each(pick, groups)
    drives = each(
        lambda p: jnp.sum(p[0:256] * p[256:257], axis=1, keepdims=True), picked
    )
    parts = each(lambda p: split(p[0:256]), picked)
    grams = each(
        lambda p: dot_nt(p[0], p[0]) + (dot_nt(p[0], p[1]) + dot_nt(p[1], p[0])), parts
    )
    grams = each(lambda g: g + jnp.where(diagonal, 255.0, 0.0), grams)
    inverses = each(
        lambda g: 1.0
        / jnp.max(jnp.sum(jnp.abs(g), axis=0, keepdims=True), axis=1, keepdims=True),
        grams,
    )
    current = each(lambda g, v: g * v, grams, inverses)
    roots = []
    for step in range(3):
        parts = each(split, current)
        second = each(square, parts)
        if step < 2:
            products = each(mul3, parts, each(split, second))
        if step != 1:
            mixed = each(lambda s, c: split(s - 4.5 * c), second, current)
            roots.append(
                each(
                    lambda m, s, c: 0.0625 * square(m)
                    + (0.421875 * s - 2.4375 * c + jnp.where(diagonal, 2.25, 0.0)),
                    mixed,
                    second,
                    current,
                )
            )
        if step < 2:
            current = each(
                lambda c, s, p: 2.25 * c - 1.5 * s + 0.25 * p, current, second, products
            )
    root = each(mul3, each(split, roots[0]), each(split, roots[1]))
    inner = each(lambda r, d: jnp.sum(r * d, axis=0, keepdims=True), root, drives)
    offsets = each(
        lambda r, n, v: jnp.sum(r * n, axis=1, keepdims=True) * v, root, inner, inverses
    )
    held = offset_ref[...]
    for u, (g, r, v, o) in enumerate(zip(groups, root, inverses, offsets)):
        root_ref[u] = jnp.sqrt(255.0 * v) * r
        held = jnp.where(lane == g, o, held)
    offset_ref[...] = held


def apply_kernel(where_ref, root_ref, offset_ref, *refs):
    pieces = refs[:MEM]
    out_ref, field, sems = refs[MEM:]
    me = where_ref[0]

    @pl.when(pl.program_id(0) == 0)
    def gather():
        copies = [
            pltpu.make_async_copy(
                pieces[s], field.at[pl.ds(pl.multiple_of((me ^ s) * 32, 32), 32), :], sems.at[s]
            )
            for s in range(MEM)
        ]
        for copy in copies:
            copy.start()
        for copy in copies:
            copy.wait()

    odd, high = lane_bits(256)
    lane = lax.broadcasted_iota(jnp.int32, (256, LANES), 1)
    groups = [pl.program_id(0) * 8 + g for g in range(8)]
    value = [field[:, pl.ds(pl.multiple_of(g * LANES, LANES), LANES)] for g in groups]
    centre = each(lambda x: jnp.sum(x, axis=0, keepdims=True) * (1.0 / 256.0), value)
    anomaly = each(lambda x, a: x - a, value, centre)
    offset = [
        jnp.sum(jnp.where(lane == g, offset_ref[...], 0.0), axis=1, keepdims=True) for g in groups
    ]
    base = each(
        lambda a, x, o: a + jnp.sum(x * o, axis=0, keepdims=True), centre, anomaly, offset
    )
    spread = each(mul3, [split(root_ref[u]) for u in range(8)], each(split, anomaly))
    mixed = each(lambda b, x: b + x, base, spread)
    for c in range(2):
        layers = exchange_lanes(mixed[4 * c : 4 * c + 4], odd, high)
        for l in range(4):
            out_ref[:, l, c * LANES : (c + 1) * LANES] = layers[l]


def find_mixing(where, nearby, damping, own, sib, far):
    return pl.pallas_call(
        mixing_kernel,
        out_shape=[
            jax.ShapeDtypeStruct((16, 256, 256), F32),
            jax.ShapeDtypeStruct((256, LANES), F32),
        ],
        grid=(16 // WIDE,),
        in_specs=[SMEM] * 3 + [ANYWHERE] * (2 + MEM),
        out_specs=[
            pl.BlockSpec((WIDE, 256, 256), lambda i: (i, 0, 0)),
            pl.BlockSpec((256, LANES), lambda i: (0, 0)),
        ],
        scratch_shapes=[
            pltpu.VMEM((256, 2176), F32),
            pltpu.VMEM((48, 264, LANES), F32),
            pltpu.SemaphoreType.DMA((MEM + 2,)),
        ],
        compiler_params=pltpu.CompilerParams(vmem_limit_bytes=42 << 20),
        cost_estimate=pl.CostEstimate(
            flops=16 * 30 * 2 * 256**3, bytes_accessed=12 << 20, transcendentals=0
        ),
        name="mixing",
    )(where, nearby, damping, own, sib, *far)


def apply_mixing(where, root, offset, pieces):
    return pl.pallas_call(
        apply_kernel,
        out_shape=jax.ShapeDtypeStruct((256, 4, 512), F32),
        grid=(2,),
        in_specs=[SMEM, pl.BlockSpec((8, 256, 256), lambda i: (i, 0, 0)), VMEM] + [ANYWHERE] * MEM,
        out_specs=pl.BlockSpec((256, 4, 2 * LANES), lambda i: (0, 0, i)),
        scratch_shapes=[pltpu.VMEM((256, 2048), F32), pltpu.SemaphoreType.DMA((MEM,))],
        compiler_params=pltpu.CompilerParams(vmem_limit_bytes=30 << 20),
        name="apply",
    )(where, root, offset, *pieces)


def send(x, flip):
    return lax.ppermute(x, "mem", [(i, i ^ flip) for i in range(MEM)])


def swap_cores(x):
    return lax.ppermute(x, "tile", [(i, i ^ 1) for i in range(32)])


def local(prior, measurement_matrix, readings, noise, nearby, damping):
    me = lax.axis_index("mem").astype(jnp.int32)
    tile = lax.axis_index("tile").astype(jnp.int32)
    where = jnp.stack([me, tile])
    measurement_map = jnp.swapaxes(measurement_matrix, 1, 2)
    *pieces, obs = local_obs(where, prior, measurement_map, readings, noise)
    hold = lax.optimization_barrier
    got = [pieces[0]] + [None] * 7
    own4, own1, own3 = send(obs, 4), send(obs, 1), send(obs, 3)
    far0 = lax.ppermute(
        obs,
        "tile",
        [(i, i + 1) for i in range(1, 31, 2)] + [(i + 1, i) for i in range(1, 31, 2)],
    )
    own5, own7, own2 = send(own4, 1), send(own4, 3), send(own3, 1)
    far4, far1, far3 = send(far0, 4), send(far0, 1), send(far0, 3)
    own6 = send(own5, 3)
    far1, far3, far4, own4 = hold((far1, far3, far4, own4))
    far5, far7 = send(far4, 1), send(far4, 3)
    table = own_table(where, (obs, own4, own1, own3, own5, own7, own2, own6))
    table, four = hold((table, pieces[4]))
    got[4] = send(four, 4)
    far2 = send(far3, 1)
    far5, far7, table, one, three = hold((far5, far7, table, pieces[1], pieces[3]))
    far6, sibling = send(far5, 3), swap_cores(table)
    got[1], got[3] = send(one, 1), send(three, 3)
    far2, sibling, got[4], *rest = hold((far2, sibling, got[4], pieces[2], *pieces[5:]))
    for s, x in zip((2, 5, 6, 7), rest):
        got[s] = send(x, s)
    far = (far0, far4, far1, far3, far5, far7, far2, far6)
    root, offset = find_mixing(where, nearby.T, damping.T, table, sibling, far)
    return apply_mixing(where, root, offset, got)


def solution(mesh):
    in_specs = (
        P("mem", None, "tile"),
        P(),
        P(("tile", "mem"), None),
        P(("tile", "mem"), None),
        P(("tile", "mem"), None),
        P(("tile", "mem"), None),
    )
    out_specs = P(None, None, ("tile", "mem"))
    return jax.shard_map(local, mesh=mesh, in_specs=in_specs, out_specs=out_specs, check_vma=False)
```
